32 devices in a mesh: dp: 8 (over z, y), mp: 4 (over x, core).
Axes of the slice: x: 2, y: 2, z: 4, core: 2. Of those that a mesh axis runs over, the one named last changes fastest.
Arguments:
- embedded_symbols: bfloat16 [4, 8192, 768], P('mp', 'dp'), may hold values from -6 to 6
- stream_opening_marker: int32 [4, 64], P('mp'), may hold values from 0 to 1, as said below
- retained_tile_selector: int32 [2, 4, 64, 15], P(None, 'mp', 'dp'), may hold values 0 or 1
- asker_projection: bfloat16 [2, 768, 768], P(None, ('dp', 'mp')), may hold values from -0.21875 to 0.21875
- lookup_projection: bfloat16 [2, 768, 768], P(None, ('dp', 'mp')), may hold values from -0.21875 to 0.21875
- content_projection: bfloat16 [2, 768, 768], P(None, ('dp', 'mp')), may hold values from -0.21875 to 0.21875
- mixer_result_projection: bfloat16 [2, 768, 768], P(None, ('dp', 'mp')), may hold values from -3.5 to 3.5
- asker_offset: bfloat16 [2, 768], P(None, ('dp', 'mp')), may hold values from -3 to 3
- content_offset: bfloat16 [2, 768], P(None, ('dp', 'mp')), may hold values from -3 to 3
- mixer_result_offset: bfloat16 [2, 768], P(None, ('dp', 'mp')), may hold values from -3 to 3
- mixer_standardise_scaling: bfloat16 [2, 768], P(None, ('dp', 'mp')), may hold values from 0.5 to 1.5
- mixer_standardise_offset: bfloat16 [2, 768], P(None, ('dp', 'mp')), may hold values from -2 to 2
- perceptron_widen_projection: bfloat16 [2, 768, 3072], P(None, ('dp', 'mp')), may hold values from -0.21875 to 0.21875
- perceptron_widen_offset: bfloat16 [2, 3072], P(None, ('dp', 'mp')), may hold values from -3 to 3
- perceptron_narrow_projection: bfloat16 [2, 3072, 768], P(None, ('dp', 'mp')), may hold values from -0.21875 to 0.21875
- perceptron_narrow_offset: bfloat16 [2, 768], P(None, ('dp', 'mp')), may hold values from -3 to 3
- perceptron_standardise_scaling: bfloat16 [2, 768], P(None, ('dp', 'mp')), may hold values from 0.5 to 1.5
- perceptron_standardise_offset: bfloat16 [2, 768], P(None, ('dp', 'mp')), may hold values from -2 to 2
- tile_gate_scores: bfloat16 [2, 768], P(None, ('dp', 'mp')), may hold values from -6 to 6
- tile_gate_jitter: bfloat16 [2, 768], P(None, ('dp', 'mp')), may hold values from -4 to 4
- relaxing_warmth: float32 [2, 12], replicated, may hold values from 0.5 to 2
- upstream_derivative: bfloat16 [4, 8192, 768], P('mp', 'dp'), may hold values from -6 to 6
Outputs:
- result: float32 [4, 8192, 768], P('mp', 'dp')
- tokens_grad: float32 [4, 8192, 768], P('mp', 'dp')
- query_proj_grad: float32 [2, 768, 768], P(None, ('dp', 'mp'))
- key_proj_grad: float32 [2, 768, 768], P(None, ('dp', 'mp'))
- value_proj_grad: float32 [2, 768, 768], P(None, ('dp', 'mp'))
- output_proj_grad: float32 [2, 768, 768], P(None, ('dp', 'mp'))
- query_bias_grad: float32 [2, 768], P(None, ('dp', 'mp'))
- value_bias_grad: float32 [2, 768], P(None, ('dp', 'mp'))
- output_bias_grad: float32 [2, 768], P(None, ('dp', 'mp'))
- first_gain_grad: float32 [2, 768], P(None, ('dp', 'mp'))
- first_shift_grad: float32 [2, 768], P(None, ('dp', 'mp'))
- inner_proj_grad: float32 [2, 768, 3072], P(None, ('dp', 'mp'))
- inner_bias_grad: float32 [2, 3072], P(None, ('dp', 'mp'))
- outer_proj_grad: float32 [2, 3072, 768], P(None, ('dp', 'mp'))
- outer_bias_grad: float32 [2, 768], P(None, ('dp', 'mp'))
- second_gain_grad: float32 [2, 768], P(None, ('dp', 'mp'))
- second_shift_grad: float32 [2, 768], P(None, ('dp', 'mp'))
- mask_logit_grad: float32 [2, 768], P(None, ('dp', 'mp'))
- new_mask: int32 [2, 768], P(None, ('dp', 'mp'))
The draws below stay inside these ranges and needn't reach their ends.
Inputs may be any that keep to these rules, and one draw needn't show every extreme that they name: `stream_opening_marker`: block 0 of each column begins a sequence; every sequence lies on one device along dp or on two neighbouring ones, with at most 4 blocks on any one device and so at most 8 blocks; every boundary between neighbouring devices along dp falls inside a sequence; in each column one sequence has exactly 8 blocks.
All inputs are finite; a program needn't handle non-finite values. No bound on the sum of `retained_tile_selector` on one device may be relied on, other than what follows from the above.
Results may differ from the reference program's by a relative error of at most 0.025.
Values may be sent and summed in bfloat16 or wider, within the bound.
No kernel may reach another device: no remote copies, remote signals or barrier semaphores. Data moves between devices by JAX's collectives and lax.ppermute only.
A program may use at most 320 MiB of HBM per device.

```python
import math
import jax
import jax.numpy as jnp
from jax import lax

D = 768
ATTENDER_TOTAL = 12
HD = 64
FF = 3072
BLK = 128
MAX_SPAN_TILES = 8
QB = 8
RIM = 4
WIN = 15
MASKW = 768
NB = 64
TCOL = 8192
N_DP = 8
N_MP = 4


def draw_stream_opening_marker(key, part):
    key = jax.random.fold_in(key, 11)
    tail_key, head_key, cut_key, edge_key = jax.random.split(key, 4)
    tails = jax.random.randint(tail_key, (N_MP, N_DP), 1, RIM + 1)
    heads = jax.random.randint(head_key, (N_MP, N_DP), 1, RIM + 1)
    edge = jax.random.randint(edge_key, (N_MP, 1), 0, N_DP - 1)
    device_ids = jnp.arange(N_DP)[None, :]
    tails = jnp.where(device_ids == edge, RIM, tails)
    heads = jnp.where(device_ids == edge + 1, RIM, heads)
    spot = jnp.arange(QB)[None, None, :]
    head_cut = heads[:, :, None]
    tail_cut = QB - tails[:, :, None]
    cuts = jax.random.randint(cut_key, (N_MP, N_DP, QB), 0, 2)
    middle = (spot > head_cut) & (spot < tail_cut) & ((cuts == 1) | ((spot - head_cut) % RIM == 0))
    opening = (spot == 0) & (jnp.arange(N_DP)[None, :, None] == 0)
    start_flags = (spot == head_cut) | (spot == tail_cut) | middle | opening
    return start_flags.astype(jnp.int32).reshape(N_MP, N_DP * QB)


def with_ends(entries, rng, low, high):
    longest = entries.shape.index(max(entries.shape))
    spots = []
    for shift in (0, 1):
        where = [jax.random.randint(jax.random.fold_in(rng, axis), (), 0, length) for axis, length in enumerate(entries.shape)]
        where[longest] = (where[longest] + shift) % entries.shape[longest]
        spots.append(tuple(where))
    return entries.at[spots[0]].set(low).at[spots[1]].set(high)


def steps_of(stream_key, dims, pieces, low, top_value):
    def one(dim, blocks):
        steps = jax.random.uniform(jax.random.fold_in(jax.random.fold_in(stream_key, 6), dim), (blocks,), jnp.float32, low / len(pieces), top_value / len(pieces))
        return jnp.repeat(jnp.exp(steps), dims[dim] // blocks).reshape((-1,) + (1,) * (len(dims) - dim - 1))

    level = one(*pieces[0])
    for cut in pieces[1:]:
        level = level * one(*cut)
    return level


def normal_values(own_key, extent, scale, reach, cuts=(), held_as=jnp.bfloat16):
    drawn = jax.random.normal(own_key, extent, jnp.float32) * scale
    if len(cuts) > 0:
        drawn = steps_of(own_key, extent, cuts, -0.22, 0.18) * drawn
    return jnp.clip(drawn, min=-reach, max=reach).astype(held_as)


def setup_inputs(seed: int = 0) -> dict:
    key_list = jax.random.split(jax.random.key(seed), 23)
    embedded_symbols = normal_values(key_list[0], (N_MP, TCOL, D), 1.0, 6.0, ((0, 4), (1, 8)))
    stream_opening_marker = draw_stream_opening_marker(jax.random.fold_in(key_list[22], 71), 0)
    retained_tile_selector = with_ends((jax.random.randint(key_list[2], (2, N_MP, NB, WIN), 0, 2) < 1).astype(jnp.int32), jax.random.fold_in(key_list[2], 1), 0, 1)
    asker_projection = normal_values(key_list[3], (2, D, D), D ** -0.5, 0.21875, ((1, 32),))
    lookup_projection = normal_values(key_list[4], (2, D, D), D ** -0.5, 0.21875, ((1, 32),))
    content_projection = normal_values(key_list[5], (2, D, D), D ** -0.5, 0.21875, ((1, 32),))
    mixer_result_projection = normal_values(key_list[6], (2, D, D), (max(1, D // 256)) ** -0.5, 3.5, ((1, 32),))
    asker_offset = normal_values(key_list[7], (2, D), 0.3, 3.0, ((1, 32),))
    content_offset = normal_values(key_list[8], (2, D), 0.3, 3.0, ((1, 32),))
    mixer_result_offset = normal_values(key_list[9], (2, D), 0.3, 3.0, ((1, 32),))
    mixer_standardise_scaling = jnp.clip(1.0 + 0.1 * jax.random.normal(key_list[10], (2, D), jnp.float32), 0.5, 1.5).astype(jnp.bfloat16)
    mixer_standardise_offset = normal_values(key_list[11], (2, D), 0.2, 2.0, ((1, 32),))
    perceptron_widen_projection = normal_values(key_list[12], (2, D, FF), D ** -0.5, 0.21875, ((1, 32),))
    perceptron_widen_offset = normal_values(key_list[13], (2, FF), 0.3, 3.0, ((1, 32),))
    perceptron_narrow_projection = normal_values(key_list[14], (2, FF, D), (FF // 4) ** -0.5, 0.21875, ((1, 32),))
    perceptron_narrow_offset = normal_values(key_list[15], (2, D), 0.3, 3.0, ((1, 32),))
    perceptron_standardise_scaling = jnp.clip(1.0 + 0.1 * jax.random.normal(key_list[16], (2, D), jnp.float32), 0.5, 1.5).astype(jnp.bfloat16)
    perceptron_standardise_offset = normal_values(key_list[17], (2, D), 0.2, 2.0, ((1, 32),))
    tile_gate_scores = normal_values(key_list[18], (2, MASKW), 1.5, 6.0, ((1, 32),))
    tile_gate_jitter = normal_values(key_list[19], (2, MASKW), 1.0, 4.0, ((1, 32),))
    relaxing_warmth = jnp.clip(jnp.exp(jax.random.uniform(key_list[20], (2, ATTENDER_TOTAL), jnp.float32, math.log(0.5), math.log(2.0))), 0.5, 2.0)
    upstream_derivative = normal_values(key_list[21], (N_MP, TCOL, D), 1.0, 6.0, ((0, 4), (1, 8)))
    return dict(embedded_symbols=embedded_symbols, stream_opening_marker=stream_opening_marker, retained_tile_selector=retained_tile_selector, asker_projection=asker_projection, lookup_projection=lookup_projection, content_projection=content_projection, mixer_result_projection=mixer_result_projection, asker_offset=asker_offset, content_offset=content_offset, mixer_result_offset=mixer_result_offset, mixer_standardise_scaling=mixer_standardise_scaling, mixer_standardise_offset=mixer_standardise_offset, perceptron_widen_projection=perceptron_widen_projection, perceptron_widen_offset=perceptron_widen_offset, perceptron_narrow_projection=perceptron_narrow_projection, perceptron_narrow_offset=perceptron_narrow_offset, perceptron_standardise_scaling=perceptron_standardise_scaling, perceptron_standardise_offset=perceptron_standardise_offset, tile_gate_scores=tile_gate_scores, tile_gate_jitter=tile_gate_jitter, relaxing_warmth=relaxing_warmth, upstream_derivative=upstream_derivative)


@jax.custom_vjp
def low(v):
    return lax.optimization_barrier(v.astype(jnp.bfloat16)).astype(jnp.float32)

@jax.custom_vjp
def low_back(v):
    return v

def low_keep(v):
    return (low(v), None)

def low_pass(kept, incoming_gradient):
    return (incoming_gradient,)

def back_keep(v):
    return (v, None)

def back_low(kept, incoming_gradient):
    return (low(incoming_gradient),)
low.defvjp(low_keep, low_pass)
low_back.defvjp(back_keep, back_low)

def matmul(left, right):
    return jnp.dot(left, right, precision=lax.Precision.HIGHEST, preferred_element_type=jnp.float32)

def norm_rows(values, gain, shift):
    middle = lax.optimization_barrier(jnp.mean(values, -1, keepdims=True))
    centred = values - middle
    spread = lax.optimization_barrier(jnp.mean(centred * centred, -1, keepdims=True))
    return centred * lax.rsqrt(spread + 1e-06) * gain + shift

def column_attention(queries, keys, values, start_flags, keep, smooth_tile_selector):
    total = start_flags.shape[0]
    order = jnp.arange(total, dtype=jnp.int32)
    seq_of = jnp.cumsum(start_flags).astype(jnp.int32) - 1
    start_of = lax.cummax(jnp.where(start_flags == 1, order, 0), axis=0)
    place_of = order - start_of
    margin = MAX_SPAN_TILES
    width = 4 + 2 * (MAX_SPAN_TILES - 1)
    key_pad = jnp.pad(keys, ((margin * BLK, margin * BLK), (0, 0)))
    value_pad = jnp.pad(values, ((margin * BLK, margin * BLK), (0, 0)))
    seq_pad = jnp.pad(seq_of, (margin, margin), constant_values=-1)
    place_pad = jnp.pad(place_of, (margin, margin))

    def group_rows(group):
        first = group * 4
        query_ids = first + jnp.arange(4, dtype=jnp.int32)
        key_first = first + margin - (MAX_SPAN_TILES - 1)
        query_rows = lax.dynamic_slice_in_dim(queries, first * BLK, 4 * BLK, 0)
        key_rows = lax.dynamic_slice_in_dim(key_pad, key_first * BLK, width * BLK, 0)
        value_rows = lax.dynamic_slice_in_dim(value_pad, key_first * BLK, width * BLK, 0)
        seq_query = seq_of[query_ids]
        seq_key = lax.dynamic_slice_in_dim(seq_pad, key_first, width, 0)
        place_query = place_of[query_ids]
        place_key = jnp.clip(lax.dynamic_slice_in_dim(place_pad, key_first, width, 0), 0, MAX_SPAN_TILES - 1)
        key_ids = first - (MAX_SPAN_TILES - 1) + jnp.arange(width, dtype=jnp.int32)
        offset = key_ids[None, :] - query_ids[:, None]
        chosen_elements = jnp.take_along_axis(keep[query_ids], jnp.clip(offset + MAX_SPAN_TILES - 1, 0, 2 * MAX_SPAN_TILES - 2), axis=1)
        kept = (seq_query[:, None] == seq_key[None, :]) & ((chosen_elements > 0) | (offset == 0))
        factor = smooth_tile_selector[:, place_query[:, None], place_key[None, :]]
        query_heads = query_rows.reshape(4 * BLK, ATTENDER_TOTAL, HD)
        key_heads = key_rows.reshape(width * BLK, ATTENDER_TOTAL, HD)
        value_heads = value_rows.reshape(width * BLK, ATTENDER_TOTAL, HD)
        scores = jnp.einsum('qhd,khd->hqk', query_heads, key_heads, precision=lax.Precision.HIGHEST) * HD ** (-0.5)
        scores = low_back(scores).reshape(ATTENDER_TOTAL, 4, BLK, width, BLK)
        masked = kept[None, :, None, :, None]
        scores = jnp.where(masked, scores, -1e+30)
        largest = lax.optimization_barrier(jnp.max(scores, axis=(3, 4), keepdims=True))
        expo = jnp.where(masked, jnp.exp(scores - largest), 0.0)
        probs = expo / lax.optimization_barrier(jnp.sum(expo, axis=(3, 4), keepdims=True))
        weights = low(probs * factor[:, :, None, :, None]).reshape(ATTENDER_TOTAL, 4 * BLK, width * BLK)
        context = jnp.einsum('hqk,khd->qhd', weights, value_heads, precision=lax.Precision.HIGHEST)
        return context.reshape(4 * BLK, ATTENDER_TOTAL * HD)
    blocks = lax.map(jax.checkpoint(group_rows), jnp.arange(total // 4, dtype=jnp.int32))
    return blocks.reshape(total * BLK, ATTENDER_TOTAL * HD)

def layer_pass(hidden_state, weights, start_flags, keep, smooth_tile_selector):
    asker_projection, lookup_projection, content_projection, mixer_result_projection, asker_offset, content_offset, mixer_result_offset, mixer_standardise_scaling, mixer_standardise_offset, perceptron_widen_projection, perceptron_widen_offset, perceptron_narrow_projection, perceptron_narrow_offset, perceptron_standardise_scaling, perceptron_standardise_offset = weights
    hidden_low = low(hidden_state)
    queries = low(low_back(matmul(hidden_low, asker_projection) + asker_offset))
    keys = low(low_back(matmul(hidden_low, lookup_projection)))
    values = low(low_back(matmul(hidden_low, content_projection) + content_offset))
    context = jax.vmap(column_attention, in_axes=(0, 0, 0, 0, 0, None))(queries, keys, values, start_flags, keep, smooth_tile_selector)
    context = low(low_back(context))
    attended = low_back(matmul(context, mixer_result_projection) + mixer_result_offset)
    normed = norm_rows(hidden_state + attended, mixer_standardise_scaling, mixer_standardise_offset)
    inner = low_back(matmul(low(normed), perceptron_widen_projection) + perceptron_widen_offset)
    active = low(jax.nn.gelu(inner, approximate=False))
    outer = low_back(matmul(active, perceptron_narrow_projection) + perceptron_narrow_offset)
    return norm_rows(normed + outer, perceptron_standardise_scaling, perceptron_standardise_offset)

def reference(embedded_symbols, stream_opening_marker, retained_tile_selector, asker_projection, lookup_projection, content_projection, mixer_result_projection, asker_offset, content_offset, mixer_result_offset, mixer_standardise_scaling, mixer_standardise_offset, perceptron_widen_projection, perceptron_widen_offset, perceptron_narrow_projection, perceptron_narrow_offset, perceptron_standardise_scaling, perceptron_standardise_offset, tile_gate_scores, tile_gate_jitter, relaxing_warmth, upstream_derivative):
    params = tuple((item.astype(jnp.float32) for item in (asker_projection, lookup_projection, content_projection, mixer_result_projection, asker_offset, content_offset, mixer_result_offset, mixer_standardise_scaling, mixer_standardise_offset, perceptron_widen_projection, perceptron_widen_offset, perceptron_narrow_projection, perceptron_narrow_offset, perceptron_standardise_scaling, perceptron_standardise_offset, tile_gate_scores)))
    score_jitter = tile_gate_jitter.astype(jnp.float32)

    def forward(inputs, weights):
        hidden_state = inputs
        for tier_evaluate in range(2):
            chosen_elements = tuple((item[tier_evaluate] for item in weights))
            smooth_tile_selector = jax.nn.sigmoid((chosen_elements[15] + score_jitter[tier_evaluate]).reshape(ATTENDER_TOTAL, MAX_SPAN_TILES, MAX_SPAN_TILES) / relaxing_warmth[tier_evaluate][:, None, None])
            hidden_state = layer_pass(hidden_state, chosen_elements[:15], stream_opening_marker, retained_tile_selector[tier_evaluate], smooth_tile_selector)
        return hidden_state
    result, pull = jax.vjp(forward, embedded_symbols.astype(jnp.float32), params)
    tokens_grad, grads = pull(upstream_derivative.astype(jnp.float32))
    new_mask = (params[15] + score_jitter > 0).astype(jnp.int32)
    return (result, tokens_grad, grads[0], grads[1], grads[2], grads[3], grads[4], grads[5], grads[6], grads[7], grads[8], grads[9], grads[10], grads[11], grads[12], grads[13], grads[14], grads[15], new_mask)
```

```python
import functools
import math

import jax
import jax.numpy as jnp
from jax import lax
from jax.experimental import pallas as pl
from jax.experimental.pallas import tpu as pltpu
from jax.sharding import PartitionSpec as P

D = 768
HEADS = 12
HD = 64
FF = 3072
BLK = 128
SPAN = 8
RIM = 4
PAIRS = HEADS // 2
AXES = ("dp", "mp")
SCALE = HD**-0.5
SCALE2 = SCALE * math.log2(math.e)
F32 = jnp.float32
BF16 = jnp.bfloat16


def cost(us):
    return pl.CostEstimate(flops=int(us * 1e9), bytes_accessed=1_000_000, transcendentals=0)


def once(shape, column=0):
    return pl.BlockSpec(shape, lambda i: (0,) * (len(shape) - 1) + (column,), pipeline_mode=pl.Buffered(1))


def dot(a, b):
    return jnp.dot(a, b, preferred_element_type=F32)


def dot_rows(a, b):
    return lax.dot_general(a, b, (((0,), (0,)), ((), ())), preferred_element_type=F32)


def dot_cols(a, b):
    return lax.dot_general(a, b, (((1,), (1,)), ((), ())), preferred_element_type=F32)


def dot_tt(a, b):
    return lax.dot_general(a, b, (((0,), (1,)), ((), ())), preferred_element_type=F32)


def scan_blocks(flags, pos, first_s, last_s, own):
    ext = own + 2 * RIM
    total = flags.shape[0]
    base = pos * own - RIM

    def opens(e):
        gid = base + e
        inside = jnp.logical_and(gid >= 0, gid < total)
        return jnp.where(inside, flags[jnp.clip(gid, 0, total - 1)], 1)

    def up(e, start):
        start = jnp.where(opens(e) == 1, e, start)
        first_s[e] = start
        return start

    lax.fori_loop(0, ext, up, jnp.int32(0))

    def down(n, stop):
        e = ext - 1 - n
        last_s[e] = stop
        return jnp.where(opens(e) == 1, e, stop)

    lax.fori_loop(0, ext, down, jnp.int32(ext))


def forward_kernel(
    flags, keep, pos, factor, q_t, k, v_t, ctx_t, lse, qbd, acc, top, total, first_s, last_s
):
    own = q_t.shape[1] // BLK
    scan_blocks(flags, pos[0], first_s, last_s, own)
    qbd[...] = jnp.zeros_like(qbd)

    @pl.loop(0, own)
    def _(i):
        cols = pl.ds(pl.multiple_of(i * BLK, BLK), BLK)
        for hp in range(PAIRS):
            qbd[hp, :HD, :BLK] = q_t[pl.ds(hp * BLK, HD), cols]
            qbd[hp, HD:, BLK:] = q_t[pl.ds(hp * BLK + HD, HD), cols]
        acc[...] = jnp.zeros_like(acc)
        top[...] = jnp.full_like(top, -1e30)
        total[...] = jnp.zeros_like(total)
        me = i + RIM
        start = first_s[me]

        @pl.loop(start, last_s[me])
        def _(e):
            wanted = jnp.logical_or(e == me, keep[i, jnp.clip(e - me + SPAN - 1, 0, 2 * SPAN - 2)] > 0)

            @pl.when(wanted)
            def _():
                rows = pl.ds(pl.multiple_of(e * BLK, BLK), BLK)
                ab = (me - start) * SPAN + (e - start)
                for hp in range(PAIRS):
                    lanes = slice(hp * BLK, (hp + 1) * BLK)
                    s = dot(k[rows, lanes], qbd[hp])
                    m_old = top[hp : hp + 1, :]
                    m_new = jnp.maximum(m_old, jnp.max(s, axis=0, keepdims=True))
                    p = jnp.exp2((s - m_new) * SCALE2)
                    alpha = jnp.exp2((m_old - m_new) * SCALE2)
                    total[hp : hp + 1, :] = total[hp : hp + 1, :] * alpha + jnp.sum(
                        p, axis=0, keepdims=True
                    )
                    top[hp : hp + 1, :] = m_new
                    c = dot(v_t[lanes, rows], p.astype(BF16))
                    f = factor[ab, hp : hp + 1, :]
                    upper = slice(hp * BLK, hp * BLK + HD)
                    lower = slice(hp * BLK + HD, (hp + 1) * BLK)
                    acc[upper, :] = acc[upper, :] * alpha[:, :BLK] + c[:HD, :BLK] * f[:, :BLK]
                    acc[lower, :] = acc[lower, :] * alpha[:, BLK:] + c[HD:, BLK:] * f[:, BLK:]

        for hp in range(PAIRS):
            t = total[hp : hp + 1, :]
            r = 1.0 / t
            upper = slice(hp * BLK, hp * BLK + HD)
            lower = slice(hp * BLK + HD, (hp + 1) * BLK)
            ctx_t[upper, cols] = acc[upper, :] * r[:, :BLK]
            ctx_t[lower, cols] = acc[lower, :] * r[:, BLK:]
            lse[i, hp : hp + 1, :] = top[hp : hp + 1, :] * SCALE2 + jnp.log2(t)


def smem():
    return pl.BlockSpec(memory_space=pltpu.SMEM)


def vmem():
    return pl.BlockSpec(memory_space=pltpu.VMEM)


def attend(flags, keep, pos, factor, q_t, k, v_t):
    own = q_t.shape[1] // BLK
    ext = own + 2 * RIM
    return pl.pallas_call(
        forward_kernel,
        out_shape=(
            jax.ShapeDtypeStruct(q_t.shape, F32),
            jax.ShapeDtypeStruct((own, 8, 2 * BLK), F32),
        ),
        in_specs=[smem(), smem(), smem(), vmem(), vmem(), vmem(), vmem()],
        out_specs=(vmem(), vmem()),
        scratch_shapes=[
            pltpu.VMEM((PAIRS, BLK, 2 * BLK), BF16),
            pltpu.VMEM((D, BLK), F32),
            pltpu.VMEM((8, 2 * BLK), F32),
            pltpu.VMEM((8, 2 * BLK), F32),
            pltpu.SMEM((ext,), jnp.int32),
            pltpu.SMEM((ext,), jnp.int32),
        ],
        compiler_params=pltpu.CompilerParams(vmem_limit_bytes=40 * 2**20),
        cost_estimate=cost(13),
        name="attend",
    )(flags, keep, pos, factor, q_t, k, v_t)


def backward_kernel(
    flags,
    keep,
    pos,
    log_factor,
    inv_factor,
    q_t,
    q,
    dc_t,
    dc,
    ctx_t,
    lse,
    k,
    k_t,
    v,
    dq_t,
    dk,
    dv,
    dr,
    qbd,
    cbd,
    q2,
    c2,
    dq_acc,
    dk_acc,
    dv_acc,
    delta,
    first_s,
    last_s,
):
    own = q_t.shape[1] // BLK
    scan_blocks(flags, pos[0], first_s, last_s, own)
    qbd[...] = jnp.zeros_like(qbd)
    cbd[...] = jnp.zeros_like(cbd)
    dk_acc[...] = jnp.zeros_like(dk_acc)
    dv_acc[...] = jnp.zeros_like(dv_acc)
    dr[...] = jnp.zeros_like(dr)
    left = lax.broadcasted_iota(jnp.int32, (BLK, BLK), 1) < HD

    @pl.loop(0, own)
    def _(i):
        cols = pl.ds(pl.multiple_of(i * BLK, BLK), BLK)
        for hp in range(PAIRS):
            lanes = slice(hp * BLK, (hp + 1) * BLK)
            upper = pl.ds(hp * BLK, HD)
            lower = pl.ds(hp * BLK + HD, HD)
            qbd[hp, :HD, :BLK] = q_t[upper, cols]
            qbd[hp, HD:, BLK:] = q_t[lower, cols]
            cu = dc_t[upper, cols]
            cl = dc_t[lower, cols]
            cbd[hp, :HD, :BLK] = cu
            cbd[hp, HD:, BLK:] = cl
            delta[hp : hp + 1, :BLK] = jnp.sum(
                cu.astype(F32) * ctx_t[upper, cols], axis=0, keepdims=True
            )
            delta[hp : hp + 1, BLK:] = jnp.sum(
                cl.astype(F32) * ctx_t[lower, cols], axis=0, keepdims=True
            )
            qn = q[cols, lanes].astype(F32)
            cn = dc[cols, lanes].astype(F32)
            q2[hp, :BLK, :] = jnp.where(left, qn, 0.0).astype(BF16)
            q2[hp, BLK:, :] = jnp.where(left, 0.0, qn).astype(BF16)
            c2[hp, :BLK, :] = jnp.where(left, cn, 0.0).astype(BF16)
            c2[hp, BLK:, :] = jnp.where(left, 0.0, cn).astype(BF16)
        dq_acc[...] = jnp.zeros_like(dq_acc)
        me = i + RIM
        start = first_s[me]

        @pl.loop(start, last_s[me])
        def _(e):
            wanted = jnp.logical_or(e == me, keep[i, jnp.clip(e - me + SPAN - 1, 0, 2 * SPAN - 2)] > 0)

            @pl.when(wanted)
            def _():
                rows = pl.ds(pl.multiple_of(e * BLK, BLK), BLK)
                ab = (me - start) * SPAN + (e - start)
                for hp in range(PAIRS):
                    lanes = slice(hp * BLK, (hp + 1) * BLK)
                    vb = v[rows, lanes]
                    s = dot(k[rows, lanes], qbd[hp])
                    dw = dot(vb, cbd[hp])
                    bias = log_factor[ab, hp : hp + 1, :] - lse[i, hp : hp + 1, :]
                    w = jnp.exp2(s * SCALE2 + bias)
                    ds = w * (dw - delta[hp : hp + 1, :] * inv_factor[ab, hp : hp + 1, :])
                    wb = w.astype(BF16)
                    dsb = ds.astype(BF16)
                    dvc = dot(wb, c2[hp])
                    dkc = dot(dsb, q2[hp])
                    dqc = dot(k_t[lanes, rows], dsb)
                    dv_acc[rows, lanes] += dvc
                    dk_acc[rows, lanes] += dkc
                    upper = slice(hp * BLK, hp * BLK + HD)
                    lower = slice(hp * BLK + HD, (hp + 1) * BLK)
                    dq_acc[upper, :] += dqc[:HD, :BLK]
                    dq_acc[lower, :] += dqc[HD:, BLK:]
                    dr[ab, hp : hp + 1, :] += jnp.sum(
                        dvc * vb.astype(F32), axis=0, keepdims=True
                    )

        dq_t[:, cols] = (dq_acc[...] * SCALE).astype(BF16)

    ext = dk.shape[0] // BLK

    @pl.loop(0, ext)
    def _(e):
        rows = pl.ds(pl.multiple_of(e * BLK, BLK), BLK)
        dk[rows, :] = (dk_acc[rows, :] * SCALE).astype(BF16)
        dv[rows, :] = dv_acc[rows, :].astype(BF16)


def attend_back(flags, keep, pos, log_factor, inv_factor, q_t, q, dc_t, dc, ctx_t, lse, k, k_t, v):
    own = q_t.shape[1] // BLK
    ext = own + 2 * RIM
    return pl.pallas_call(
        backward_kernel,
        out_shape=(
            jax.ShapeDtypeStruct(q_t.shape, BF16),
            jax.ShapeDtypeStruct(k.shape, BF16),
            jax.ShapeDtypeStruct(v.shape, BF16),
            jax.ShapeDtypeStruct((SPAN * SPAN, 8, BLK), F32),
        ),
        in_specs=[smem()] * 3 + [vmem()] * 11,
        out_specs=(vmem(),) * 4,
        scratch_shapes=[
            pltpu.VMEM((PAIRS, BLK, 2 * BLK), BF16),
            pltpu.VMEM((PAIRS, BLK, 2 * BLK), BF16),
            pltpu.VMEM((PAIRS, 2 * BLK, BLK), BF16),
            pltpu.VMEM((PAIRS, 2 * BLK, BLK), BF16),
            pltpu.VMEM((D, BLK), F32),
            pltpu.VMEM((ext * BLK, D), F32),
            pltpu.VMEM((ext * BLK, D), F32),
            pltpu.VMEM((8, 2 * BLK), F32),
            pltpu.SMEM((ext,), jnp.int32),
            pltpu.SMEM((ext,), jnp.int32),
        ],
        compiler_params=pltpu.CompilerParams(vmem_limit_bytes=56 * 2**20),
        cost_estimate=cost(5),
        name="attend_back",
    )(flags, keep, pos, log_factor, inv_factor, q_t, q, dc_t, dc, ctx_t, lse, k, k_t, v)


def centred_rows(x):
    middle = jnp.mean(x, -1, keepdims=True)
    c = x - middle
    spread = jnp.mean(c * c, -1, keepdims=True)
    r = lax.rsqrt(spread + 1e-06)
    return c * r, r

def gelu_and_slope(v):
    e = jnp.exp2(v * v * (-0.5 * math.log2(math.e)))
    t = 1.0 / (1.0 + jnp.abs(v) * (0.3275911 * math.sqrt(0.5)))
    q = t * (0.127414796 + t * (-0.142248368 + t * (0.7107068705 + t * (-0.7265760135 + t * 0.5307027145)))) * e
    phi = jnp.where(v >= 0, 1.0 - q, q)
    return v * phi, phi + v * (e * (1.0 / math.sqrt(2.0 * math.pi)))

ROWS = 256

def ffn_kernel(ctx_t, hidden, wo, w1, w2, vec, b1, first, normed_low, active, slope, second, result, result_low):
    x = hidden[...].astype(F32) + dot_rows(ctx_t[...].astype(BF16), wo[...]) + vec[0:1, :]
    first[...] = x
    hat, _ = centred_rows(x)
    normed = hat * vec[1:2, :] + vec[2:3, :]
    low = normed.astype(BF16)
    normed_low[...] = low
    total = normed + vec[3:4, :]
    for j in range(FF // D):
        cols = slice(j * D, (j + 1) * D)
        inner = dot(low, w1[:, cols]) + b1[:, cols]
        a, s = gelu_and_slope(inner)
        a = a.astype(BF16)
        active[:, cols] = a
        slope[:, cols] = s.astype(BF16)
        total = total + dot(a, w2[:, cols])
    second[...] = total
    hat, _ = centred_rows(total)
    x = hat * vec[4:5, :] + vec[5:6, :]
    result[...] = x
    result_low[...] = x.astype(BF16)

def ffn(ctx_t, hidden, wo, wo_at, w12, vec, b1):
    n = hidden.shape[0]
    row = lambda w: pl.BlockSpec((ROWS, w), lambda i: (i, 0))
    return pl.pallas_call(
        ffn_kernel,
        grid=(n // ROWS,),
        in_specs=[pl.BlockSpec((D, ROWS), lambda i: (0, i)), row(D), once((D, D), wo_at), once((D, FF)), once((D, FF), 1), once((8, D)), once((1, FF))],
        out_specs=[row(D), row(D), row(FF), row(FF), row(D), row(D), row(D)],
        out_shape=[jax.ShapeDtypeStruct((n, D), F32), jax.ShapeDtypeStruct((n, D), BF16), jax.ShapeDtypeStruct((n, FF), BF16),
                   jax.ShapeDtypeStruct((n, FF), BF16), jax.ShapeDtypeStruct((n, D), F32), jax.ShapeDtypeStruct((n, D), F32), jax.ShapeDtypeStruct((n, D), BF16)],
        compiler_params=pltpu.CompilerParams(vmem_limit_bytes=56 * 2**20),
        cost_estimate=cost(28),
        name="ffn",
    )(ctx_t, hidden, wo, w12, w12, vec, b1)

def ffn_back_kernel(grad, second, first, slope, w1, w2, wo, gains, douter, dinner, dfirst, dattend, dc, dc_t, sums, b1_sum):
    @pl.when(pl.program_id(0) == 0)
    def _():
        sums[...] = jnp.zeros_like(sums)
        b1_sum[...] = jnp.zeros_like(b1_sum)
    def back(g, x, gain):
        hat, r = centred_rows(x)
        e = g * gain
        return (e - jnp.mean(e, -1, keepdims=True) - hat * jnp.mean(e * hat, -1, keepdims=True)) * r, hat
    def column(v):
        return jnp.sum(v, 0, keepdims=True)
    g = grad[...].astype(F32)
    dsecond, hat = back(g, second[...], gains[4:5, :])
    sums[0:1, :] += column(g * hat)
    sums[1:2, :] += column(g)
    low = dsecond.astype(BF16)
    douter[...] = low
    sums[2:3, :] += column(low.astype(F32))
    dnormed = dsecond
    for j in range(FF // D):
        cols = slice(j * D, (j + 1) * D)
        d = (dot_cols(low, w2[:, cols]) * slope[:, cols].astype(F32)).astype(BF16)
        dinner[:, cols] = d
        b1_sum[:, cols] += column(d.astype(F32))
        dnormed = dnormed + dot_cols(d, w1[:, cols])
    dx, hat = back(dnormed, first[...], gains[1:2, :])
    sums[3:4, :] += column(dnormed * hat)
    sums[4:5, :] += column(dnormed)
    dfirst[...] = dx
    low = dx.astype(BF16)
    dattend[...] = low
    sums[5:6, :] += column(low.astype(F32))
    dc[...] = dot_cols(low, wo[...]).astype(BF16)
    dc_t[...] = dot_cols(wo[...], low).astype(BF16)

def ffn_back(grad, second, first, slope, w12, wo, wo_at, gains):
    n = grad.shape[0]
    row = lambda w: pl.BlockSpec((ROWS, w), lambda i: (i, 0))
    return pl.pallas_call(
        ffn_back_kernel,
        grid=(n // ROWS,),
        in_specs=[row(D), row(D), row(D), row(FF), once((D, FF)), once((D, FF), 1), once((D, D), wo_at), once((8, D))],
        out_specs=[row(D), row(FF), row(D), row(D), row(D), pl.BlockSpec((D, ROWS), lambda i: (0, i)), pl.BlockSpec((8, D), lambda i: (0, 0)), pl.BlockSpec((1, FF), lambda i: (0, 0))],
        out_shape=[jax.ShapeDtypeStruct((n, D), BF16), jax.ShapeDtypeStruct((n, FF), BF16), jax.ShapeDtypeStruct((n, D), F32),
                   jax.ShapeDtypeStruct((n, D), BF16), jax.ShapeDtypeStruct((n, D), BF16), jax.ShapeDtypeStruct((D, n), BF16),
                   jax.ShapeDtypeStruct((8, D), F32), jax.ShapeDtypeStruct((1, FF), F32)],
        compiler_params=pltpu.CompilerParams(vmem_limit_bytes=56 * 2**20),
        cost_estimate=cost(23),
        name="ffn_back",
    )(grad, second, first, slope, w12, w12, wo, gains)

def ffn_grads_kernel(normed, dinner, active, douter, ctx_t, dattend, sums, b1_sum, out, turned):
    n = pl.program_id(0)
    blocks = FF // D
    @pl.when(n == 0)
    def _():
        turned[...] = normed[...].T
    @pl.when(n < blocks)
    def _():
        out[...] = dot(turned[...], dinner[...]).astype(BF16)
    @pl.when(jnp.logical_and(n >= blocks, n < 2 * blocks))
    def _():
        out[...] = dot_rows(active[...], douter[...]).astype(BF16)
    @pl.when(n == 2 * blocks)
    def _():
        out[...] = dot(ctx_t[...].astype(BF16), dattend[...]).astype(BF16)
    @pl.when(n == 2 * blocks + 1)
    def _():
        rows = jnp.concatenate([sums[...]] + [b1_sum[:, j * D:(j + 1) * D] for j in range(blocks)] + [jnp.zeros((128 - 8 - blocks, D), F32)], 0)
        out[:, :128] = rows.T.astype(BF16)

def ffn_grads(normed, dinner, active, douter, ctx_t, dattend, sums, b1_sum):
    n = normed.shape[0]
    blocks = FF // D
    return pl.pallas_call(
        ffn_grads_kernel,
        grid=(2 * blocks + 2,),
        in_specs=[once((n, D)), pl.BlockSpec((n, D), lambda i: (0, jnp.minimum(i, blocks - 1))),
                  pl.BlockSpec((n, D), lambda i: (0, jnp.clip(i - blocks, 0, blocks - 1))),
                  once((n, D)), once((D, n)), once((n, D)), once((8, D)), once((1, FF))],
        out_specs=pl.BlockSpec((D, D), lambda i: (0, i)),
        out_shape=jax.ShapeDtypeStruct((D, 2 * FF + D + 128), BF16),
        scratch_shapes=[pltpu.VMEM((D, n), BF16)],
        compiler_params=pltpu.CompilerParams(vmem_limit_bytes=56 * 2**20),
        cost_estimate=cost(20),
        name="ffn_grads",
    )(normed, dinner, active, douter, ctx_t, dattend, sums, b1_sum)


def project_kernel(low, w, qb, vb, q, q_t, k, k_t, v, v_t):
    i = pl.program_id(0)
    n = pl.num_programs(0)
    x = low[...]
    kk = dot(x, w[:, D : 2 * D]).astype(BF16)
    k[...] = kk
    k_t[...] = kk.T
    vv = (dot(x, w[:, 2 * D : 3 * D]) + vb[...]).astype(BF16)
    v[...] = vv
    v_t[...] = vv.T
    skip = RIM * BLK // ROWS

    @pl.when(jnp.logical_and(i >= skip, i < n - skip))
    def _():
        qq = (dot(x, w[:, :D]) + qb[...]).astype(BF16)
        q[...] = qq
        q_t[...] = qq.T

def project(low_ext, w, qb, vb):
    n = low_ext.shape[0]
    rim = RIM * BLK
    skip = rim // ROWS
    own = n - 2 * rim
    last = own // ROWS - 1
    row = pl.BlockSpec((ROWS, D), lambda i: (i, 0))
    col = pl.BlockSpec((D, ROWS), lambda i: (0, i))
    qrow = pl.BlockSpec((ROWS, D), lambda i: (jnp.clip(i - skip, 0, last), 0))
    qcol = pl.BlockSpec((D, ROWS), lambda i: (0, jnp.clip(i - skip, 0, last)))
    tall = jax.ShapeDtypeStruct((n, D), BF16)
    wide = jax.ShapeDtypeStruct((D, n), BF16)
    return pl.pallas_call(
        project_kernel,
        grid=(n // ROWS,),
        in_specs=[row, once((D, 3 * D)), once((1, D)), once((1, D))],
        out_specs=[qrow, qcol, row, col, row, col],
        out_shape=[jax.ShapeDtypeStruct((own, D), BF16), jax.ShapeDtypeStruct((D, own), BF16), tall, wide, tall, wide],
        compiler_params=pltpu.CompilerParams(vmem_limit_bytes=40 * 2**20),
        cost_estimate=cost(14),
        name="project",
    )(low_ext, w, qb, vb)

def att_grads_kernel(low, dq_t, dk, dv, logit, out, turned):
    n = pl.program_id(0)
    own = dq_t.shape[1]
    rim = (low.shape[0] - own) // 2

    @pl.when(n == 0)
    def _():
        turned[...] = low[...].T
        out[...] = dot_cols(turned[:, rim : rim + own], dq_t[...]).astype(BF16)

    @pl.when(n == 1)
    def _():
        out[...] = dot(turned[...], dk[...]).astype(BF16)

    @pl.when(n == 2)
    def _():
        out[...] = dot(turned[...], dv[...]).astype(BF16)

    @pl.when(n == 3)
    def _():
        qb = jnp.sum(dq_t[...].astype(F32), 1, keepdims=True)
        vb = jnp.sum(dv[...].astype(F32), 0, keepdims=True)
        rows = jnp.concatenate([vb, logit[...], jnp.zeros((126, D), F32)], 0).T
        lane = lax.broadcasted_iota(jnp.int32, (D, 128), 1)
        out[:, :128] = jnp.where(lane == 2, qb, rows).astype(BF16)

def att_grads(low_ext, dq_t, dk, dv, logit):
    n = low_ext.shape[0]
    own = dq_t.shape[1]
    return pl.pallas_call(
        att_grads_kernel,
        grid=(4,),
        in_specs=[once((n, D)), once((D, own)), once((n, D)), once((n, D)), once((1, D))],
        out_specs=pl.BlockSpec((D, D), lambda i: (0, i)),
        out_shape=jax.ShapeDtypeStruct((D, 3 * D + 128), BF16),
        scratch_shapes=[pltpu.VMEM((D, n), BF16)],
        compiler_params=pltpu.CompilerParams(vmem_limit_bytes=48 * 2**20),
        cost_estimate=cost(12),
        name="att_grads",
    )(low_ext, dq_t, dk, dv, logit)

def input_back_kernel(dk, dv, dq_t, dfirst, w, own, rims):
    i = pl.program_id(0)
    n = pl.num_programs(0)
    skip = RIM * BLK // ROWS
    total = dot_cols(dk[...], w[:, D : 2 * D]) + dot_cols(dv[...], w[:, 2 * D : 3 * D])
    inside = jnp.logical_and(i >= skip, i < n - skip)

    @pl.when(inside)
    def _():
        own[...] = total + dot_tt(dq_t[...], w[:, :D]) + dfirst[...]

    @pl.when(jnp.logical_not(inside))
    def _():
        rims[...] = total.astype(BF16)

def input_back(dk, dv, dq_t, dfirst, w):
    n = dk.shape[0]
    own = dfirst.shape[0]
    skip = (n - own) // 2 // ROWS
    last = own // ROWS - 1
    row = pl.BlockSpec((ROWS, D), lambda i: (i, 0))
    orow = pl.BlockSpec((ROWS, D), lambda i: (jnp.clip(i - skip, 0, last), 0))
    ocol = pl.BlockSpec((D, ROWS), lambda i: (0, jnp.clip(i - skip, 0, last)))
    rrow = pl.BlockSpec((ROWS, D), lambda i: (jnp.where(i < skip, i, jnp.maximum(i - last - 1, skip)), 0))
    return pl.pallas_call(
        input_back_kernel,
        grid=(n // ROWS,),
        in_specs=[row, row, ocol, orow, once((D, 3 * D))],
        out_specs=[orow, rrow],
        out_shape=[jax.ShapeDtypeStruct((own, D), F32), jax.ShapeDtypeStruct((n - own, D), BF16)],
        compiler_params=pltpu.CompilerParams(vmem_limit_bytes=40 * 2**20),
        cost_estimate=cost(12),
        name="input_back",
    )(dk, dv, dq_t, dfirst, w)


def neighbours(tail, head):
    count = lax.axis_size("dp")
    return (
        lax.ppermute(tail, "dp", [(i, i + 1) for i in range(count - 1)]),
        lax.ppermute(head, "dp", [(i + 1, i) for i in range(count - 1)]),
    )


def gathered(part):
    return lax.all_gather(part, AXES, axis=0, tiled=True)


def place():
    dp = lax.axis_index("dp")
    mp = lax.axis_index("mp")
    return dp // 2, (dp % 2) * (lax.axis_size("mp") // 2) + mp // 2, mp % 2


def sizes():
    return lax.axis_size("dp") // 2, lax.axis_size("mp")


def swap(block, mask):
    count = lax.axis_size("dp") * lax.axis_size("mp")
    return lax.ppermute(block, AXES, [(i, i ^ mask) for i in range(count)])


def gathered_in_steps(part):
    far, middle = sizes()
    z, m, c = place()
    plane = jnp.zeros((far,) + part.shape, part.dtype)
    for d in range(far):
        piece = part if d == 0 else swap(part, d * 2 * middle)
        plane = lax.dynamic_update_slice(plane, piece[None], (z ^ d, 0, 0))
    half = jnp.zeros((middle,) + plane.shape, part.dtype)
    for d in range(middle):
        piece = plane if d == 0 else swap(plane, d * 2)
        half = lax.dynamic_update_slice(half, piece[None], (m ^ d, 0, 0, 0))
    other = swap(half, 1)
    whole = jnp.zeros((2,) + half.shape, part.dtype)
    whole = lax.dynamic_update_slice(whole, half[None], (c, 0, 0, 0, 0))
    whole = lax.dynamic_update_slice(whole, other[None], (1 - c, 0, 0, 0, 0))
    return whole.transpose(2, 1, 0, 3, 4).reshape(-1, part.shape[1])


def scattered(part):
    return lax.psum_scatter(part, AXES, scatter_dimension=0, tiled=True).astype(F32)


def pick(array, index, axis):
    return lax.dynamic_index_in_dim(array, index, axis, keepdims=False)


class SteppedSum:
    def __init__(self, part):
        far, middle = sizes()
        self.parts = part.reshape(far, middle, 2, -1, part.shape[1])
        self.step = 0

    def middle_sum(self, index):
        kept, got = self.halves
        return pick(kept, index, 1).astype(F32) + pick(got, index, 1).astype(F32)

    def far_sum(self, index):
        z, m, c = place()
        total = self.middle_own(index)
        for piece in self.arrived:
            total = total + pick(piece, index, 0).astype(F32)
        return total

    def middle_own(self, index):
        z, m, c = place()
        kept, got = self.halves
        return pick(pick(kept, m, 1), index, 0).astype(F32) + pick(
            pick(got, m, 1), index, 0
        ).astype(F32)

    def advance(self, tied):
        far, middle = sizes()
        z, m, c = place()
        self.step += 1
        if self.step == 1:
            out = pick(self.parts, 1 - c, 2)
            tied, out = lax.optimization_barrier((tied, out))
            self.halves = (pick(self.parts, c, 2), swap(out, 1))
        elif self.step == 2:
            out = [self.middle_sum(m ^ d).astype(BF16) for d in range(1, middle)]
            tied, out = lax.optimization_barrier((tied, out))
            self.arrived = [swap(item, d * 2) for d, item in zip(range(1, middle), out)]
        else:
            out = [self.far_sum(z ^ d).astype(BF16) for d in range(1, far)]
            tied, out = lax.optimization_barrier((tied, out))
            self.last = [swap(item, d * 2 * middle) for d, item in zip(range(1, far), out)]
        return tied

    def result(self):
        z, m, c = place()
        total = self.far_sum(z)
        for piece in self.last:
            total = total + piece.astype(F32)
        return total


def table_rows(table):
    rows = table.reshape(PAIRS, 2, SPAN * SPAN).transpose(2, 0, 1)
    return jnp.repeat(rows, BLK, axis=2)


def layer_forward(hidden, low_ext, head, vec, flags, keep, temper, pos, between):
    z = (vec["logits"] + vec["jitter"]).reshape(HEADS, SPAN, SPAN) / temper[:, None, None]
    relaxed = jax.nn.sigmoid(z)
    factor = table_rows(relaxed)
    q, q_t, k, k_t, v, v_t = project(low_ext, head, vec["qb"][None], vec["vb"][None])
    ctx_t, lse = attend(flags, keep, pos, factor, q_t, k, v_t)
    ctx_t, wo, wo_at, w12 = between(ctx_t)
    names = ("ob", "g1", "s1", "b2", "g2", "s2", "s2", "s2")
    vectors = jnp.stack([vec[name] for name in names])
    first, normed_low, active, slope, second, result, result_low = ffn(
        ctx_t, hidden, wo, wo_at, w12, vectors, vec["b1"][None]
    )
    record = (low_ext, q, q_t, k, k_t, v, ctx_t, lse, first, normed_low, active, slope, second)
    return result, result_low, record + (relaxed, factor, vectors, head, wo, wo_at, w12)


def layer_backward(grad, record, flags, keep, temper, pos, before=None, done=None):
    low_ext, q, q_t, k, k_t, v, ctx_t, lse, first, normed_low, active, slope, second = record[:13]
    relaxed, factor, vectors, head, wo, wo_at, w12 = record[13:]
    rows = first.shape[0]
    rim = RIM * BLK
    if before is not None:
        grad = before.advance(grad)
    douter, dinner, dfirst, dattend, dc, dc_t, row_sums, b1_sum = ffn_back(
        grad, second, first, slope, w12, wo, wo_at, vectors
    )
    ffn_part = ffn_grads(normed_low, dinner, active, douter, ctx_t, dattend, row_sums, b1_sum)
    if before is None:
        dc, ffn_part = lax.optimization_barrier((dc, ffn_part))
        ffn_sum = scattered(ffn_part)
    else:
        dc, done = lax.optimization_barrier((dc, done))
        dc = before.advance(dc)
        ffn_sum = SteppedSum(ffn_part)
        dc = ffn_sum.advance(dc)
        dc = before.advance(dc)
        dc = ffn_sum.advance(dc)
    dq_t, dk, dv, dr = attend_back(
        flags, keep, pos, jnp.log2(factor), 1.0 / factor, q_t, q, dc_t, dc, ctx_t, lse, k, k_t, v
    )
    drelaxed = dr[:, :PAIRS].reshape(SPAN * SPAN, HEADS, HD).sum(-1).T.reshape(HEADS, SPAN, SPAN)
    logit_grad = (drelaxed * (1.0 - relaxed) / temper[:, None, None]).reshape(1, -1)
    if before is None:
        own, rims = input_back(dk, dv, dq_t, dfirst, head)
        from_lower, from_upper = neighbours(rims[rim:], rims[:rim])
        dq_t, rims = lax.optimization_barrier((dq_t, rims))
        att_sum = SteppedSum(att_grads(low_ext, dq_t, dk, dv, logit_grad))
    else:
        att_sum = SteppedSum(att_grads(low_ext, dq_t, dk, dv, logit_grad))
        dk = att_sum.advance(dk)
        dk = ffn_sum.advance(dk)
        own, rims = input_back(dk, dv, dq_t, dfirst, head)
        own = att_sum.advance(own)
        from_lower, from_upper = neighbours(rims[rim:], rims[:rim])
        own = att_sum.advance(own)
    dhidden = own.at[:rim].add(from_lower.astype(F32))
    dhidden = dhidden.at[rows - rim :].add(from_upper.astype(F32))
    return dhidden, ffn_sum, att_sum, done


def per_device(
    embedded,
    opening,
    selector,
    wq,
    wk,
    wv,
    wo,
    qb,
    vb,
    ob,
    g1,
    s1,
    w1,
    b1,
    w2,
    b2,
    g2,
    s2,
    scores,
    jitter,
    warmth,
    upstream,
):
    share = wq.shape[1]
    devices = D // share
    flags = opening[0]
    pos = lax.axis_index("dp").reshape(1).astype(jnp.int32)
    rim = RIM * BLK

    def widened(part):
        lead = part.shape[:-1]
        return jnp.swapaxes(part.reshape(lead + (devices, 4, share)), -3, -2).reshape(lead + (FF,))

    def unwidened(part):
        lead = part.shape[:-1]
        return jnp.swapaxes(part.reshape(lead + (4, devices, share)), -3, -2).reshape(lead + (FF,))

    def own_parts(tier):
        narrow = w2[tier].reshape(4, share, D)
        vectors = jnp.stack(
            [item[tier] for item in (qb, vb, ob, g1, s1, b2, g2, s2, scores, jitter)]
            + [b1[tier].reshape(4, share)[j] for j in range(4)],
            1,
        )
        vectors = jnp.pad(vectors, ((0, 0), (0, 128 - vectors.shape[1])))
        first = [wq[tier], wk[tier], wv[tier]]
        wide = [widened(w1[tier])] + [narrow[j] for j in range(4)]
        return first, wide, [wo[tier]], [vectors]

    def unpacked(columns):
        columns = jnp.transpose(columns.astype(F32))
        names = ("qb", "vb", "ob", "g1", "s1", "b2", "g2", "s2", "logits", "jitter")
        vec = {name: columns[n] for n, name in enumerate(names)}
        vec["b1"] = columns[len(names) : len(names) + 4].reshape(FF)
        return vec

    symbols = embedded[0]
    lower, upper = neighbours(symbols[symbols.shape[0] - rim :], symbols[:rim])
    low_ext = jnp.concatenate([lower, symbols, upper], 0)
    first, wide, out, vectors = own_parts(0)
    head_zero = gathered_in_steps(jnp.concatenate(first + vectors, 1))
    head_zero, *rest = lax.optimization_barrier((head_zero, *wide, *out))
    tail_zero = gathered(jnp.concatenate(rest, 1))
    later = {}

    def between_zero(ctx_t):
        first, wide, out, vectors = own_parts(1)
        ctx_t, tail, *parts = lax.optimization_barrier(
            (ctx_t, tail_zero, *first, *out, *vectors, *wide)
        )
        later["head"] = gathered_in_steps(jnp.concatenate(parts[:5], 1))
        later["tail"] = gathered(jnp.concatenate(parts[5:], 1))
        return ctx_t, tail, 2 * FF // D, tail

    def between_one(ctx_t):
        return ctx_t, later["head"], 3, later["tail"]

    hidden, low, record = layer_forward(
        symbols,
        low_ext,
        head_zero,
        unpacked(head_zero[:, 3 * D :]),
        flags,
        selector[0, 0],
        warmth[0],
        pos,
        between_zero,
    )
    records = [record]
    lower, upper = neighbours(low[low.shape[0] - rim :], low[:rim])
    low_ext = jnp.concatenate([lower, low, upper], 0)
    hidden, _, record = layer_forward(
        hidden,
        low_ext,
        later["head"],
        unpacked(later["head"][:, 4 * D :]),
        flags,
        selector[1, 0],
        warmth[1],
        pos,
        between_one,
    )
    records.append(record)
    grad = upstream[0]
    grad, ffn_one, att_one, _ = layer_backward(
        grad, records[1], flags, selector[1, 0], warmth[1], pos
    )
    grad, ffn_zero, att_zero, ffn_one = layer_backward(
        grad, records[0], flags, selector[0, 0], warmth[0], pos, att_one, ffn_one
    )
    sums = jnp.stack(
        [
            jnp.concatenate([ffn_zero.result(), att_zero.result()], 1),
            jnp.concatenate([ffn_one, att_one.result()], 1),
        ]
    )
    w1_grad = unwidened(sums[:, :, :FF])
    w2_grad = jnp.concatenate([sums[:, :, FF + j * D : FF + (j + 1) * D] for j in range(4)], 1)
    wo_grad = sums[:, :, 2 * FF : 2 * FF + D]
    fv = sums[:, :, 2 * FF + D : 2 * FF + D + 128]
    att = sums[:, :, 2 * FF + D + 128 :]
    av = att[:, :, 3 * D :]
    b1_grad = jnp.concatenate([fv[:, :, 8 + j] for j in range(4)], 1)
    new_mask = (scores.astype(F32) + jitter.astype(F32) > 0).astype(jnp.int32)
    return (
        hidden[None],
        grad[None],
        att[:, :, :D],
        att[:, :, D : 2 * D],
        att[:, :, 2 * D : 3 * D],
        wo_grad,
        av[:, :, 2],
        av[:, :, 0],
        fv[:, :, 5],
        fv[:, :, 3],
        fv[:, :, 4],
        w1_grad,
        b1_grad,
        w2_grad,
        fv[:, :, 2],
        fv[:, :, 0],
        fv[:, :, 1],
        av[:, :, 1],
        new_mask,
    )


def solution(mesh):
    rows = P("mp", "dp", None)
    matrix = P(None, AXES, None)
    vector = P(None, AXES)
    return jax.shard_map(
        per_device,
        mesh=mesh,
        in_specs=(rows, P("mp", None), P(None, "mp", "dp", None))
        + (matrix,) * 4
        + (vector,) * 5
        + (matrix, vector, matrix)
        + (vector,) * 5
        + (P(), rows),
        out_specs=(rows, rows)
        + (matrix,) * 4
        + (vector,) * 5
        + (matrix, vector, matrix)
        + (vector,) * 5,
        check_vma=False,
    )
```

```python
import functools
import math

import jax
import jax.numpy as jnp
from jax import lax
from jax.experimental import pallas as pl
from jax.experimental.pallas import tpu as pltpu
from jax.sharding import PartitionSpec as P

D = 768
HEADS = 12
HD = 64
FF = 3072
BLK = 128
SPAN = 8
RIM = 4
PAIRS = HEADS // 2
AXES = ("dp", "mp")
SCALE = HD**-0.5
SCALE2 = SCALE * math.log2(math.e)
F32 = jnp.float32
BF16 = jnp.bfloat16


def cost(us):
    return pl.CostEstimate(flops=int(us * 1e9), bytes_accessed=1_000_000, transcendentals=0)


def once(shape, column=0):
    return pl.BlockSpec(shape, lambda i: (0,) * (len(shape) - 1) + (column,), pipeline_mode=pl.Buffered(1))


def dot(a, b):
    return jnp.dot(a, b, preferred_element_type=F32)


def dot_rows(a, b):
    return lax.dot_general(a, b, (((0,), (0,)), ((), ())), preferred_element_type=F32)


def dot_cols(a, b):
    return lax.dot_general(a, b, (((1,), (1,)), ((), ())), preferred_element_type=F32)


def dot_tt(a, b):
    return lax.dot_general(a, b, (((0,), (1,)), ((), ())), preferred_element_type=F32)


def scan_blocks(flags, pos, first_s, last_s, own):
    ext = own + 2 * RIM
    total = flags.shape[0]
    base = pos * own - RIM

    def opens(e):
        gid = base + e
        inside = jnp.logical_and(gid >= 0, gid < total)
        return jnp.where(inside, flags[jnp.clip(gid, 0, total - 1)], 1)

    def up(e, start):
        start = jnp.where(opens(e) == 1, e, start)
        first_s[e] = start
        return start

    lax.fori_loop(0, ext, up, jnp.int32(0))

    def down(n, stop):
        e = ext - 1 - n
        last_s[e] = stop
        return jnp.where(opens(e) == 1, e, stop)

    lax.fori_loop(0, ext, down, jnp.int32(ext))


def list_kept(keep, i, first_s, last_s, kept_s):
    me = i + RIM

    def one(e, count):
        wanted = jnp.logical_or(e == me, keep[i, jnp.clip(e - me + SPAN - 1, 0, 2 * SPAN - 2)] > 0)

        @pl.when(wanted)
        def _():
            kept_s[count] = e

        return count + wanted.astype(jnp.int32)

    return lax.fori_loop(first_s[me], last_s[me], one, jnp.int32(0))


def two_kept(n, count, kept_s, start, me):
    out = []
    for e in (kept_s[2 * n], kept_s[jnp.minimum(2 * n + 1, count - 1)]):
        rows = pl.ds(pl.multiple_of(e * BLK, BLK), BLK)
        out.append((rows, (me - start) * SPAN + (e - start)))
    void = jnp.where(2 * n + 1 < count, 0.0, -1e30).astype(F32)
    return out, void


def forward_kernel(
    flags, keep, pos, factor, q_t, k, v_t, ctx_t, lse, qbd, acc, top, total, first_s, last_s
):
    own = q_t.shape[1] // BLK
    scan_blocks(flags, pos[0], first_s, last_s, own)
    qbd[...] = jnp.zeros_like(qbd)

    @pl.loop(0, own)
    def _(i):
        cols = pl.ds(pl.multiple_of(i * BLK, BLK), BLK)
        for hp in range(PAIRS):
            qbd[hp, :HD, :BLK] = q_t[pl.ds(hp * BLK, HD), cols]
            qbd[hp, HD:, BLK:] = q_t[pl.ds(hp * BLK + HD, HD), cols]
        acc[...] = jnp.zeros_like(acc)
        top[...] = jnp.full_like(top, -1e30)
        total[...] = jnp.zeros_like(total)
        me = i + RIM
        start = first_s[me]

        @pl.loop(start, last_s[me])
        def _(e):
            wanted = jnp.logical_or(e == me, keep[i, jnp.clip(e - me + SPAN - 1, 0, 2 * SPAN - 2)] > 0)

            @pl.when(wanted)
            def _():
                rows = pl.ds(pl.multiple_of(e * BLK, BLK), BLK)
                ab = (me - start) * SPAN + (e - start)
                for hp in range(PAIRS):
                    lanes = slice(hp * BLK, (hp + 1) * BLK)
                    s = dot(k[rows, lanes], qbd[hp])
                    m_old = top[hp : hp + 1, :]
                    m_new = jnp.maximum(m_old, jnp.max(s, axis=0, keepdims=True))
                    p = jnp.exp2((s - m_new) * SCALE2)
                    alpha = jnp.exp2((m_old - m_new) * SCALE2)
                    total[hp : hp + 1, :] = total[hp : hp + 1, :] * alpha + jnp.sum(
                        p, axis=0, keepdims=True
                    )
                    top[hp : hp + 1, :] = m_new
                    c = dot(v_t[lanes, rows], p.astype(BF16))
                    f = factor[ab, hp : hp + 1, :]
                    upper = slice(hp * BLK, hp * BLK + HD)
                    lower = slice(hp * BLK + HD, (hp + 1) * BLK)
                    acc[upper, :] = acc[upper, :] * alpha[:, :BLK] + c[:HD, :BLK] * f[:, :BLK]
                    acc[lower, :] = acc[lower, :] * alpha[:, BLK:] + c[HD:, BLK:] * f[:, BLK:]

        for hp in range(PAIRS):
            t = total[hp : hp + 1, :]
            r = 1.0 / t
            upper = slice(hp * BLK, hp * BLK + HD)
            lower = slice(hp * BLK + HD, (hp + 1) * BLK)
            ctx_t[upper, cols] = acc[upper, :] * r[:, :BLK]
            ctx_t[lower, cols] = acc[lower, :] * r[:, BLK:]
            lse[i, hp : hp + 1, :] = top[hp : hp + 1, :] * SCALE2 + jnp.log2(t)


def smem():
    return pl.BlockSpec(memory_space=pltpu.SMEM)


def vmem():
    return pl.BlockSpec(memory_space=pltpu.VMEM)


def attend(flags, keep, pos, factor, q_t, k, v_t):
    own = q_t.shape[1] // BLK
    ext = own + 2 * RIM
    return pl.pallas_call(
        forward_kernel,
        out_shape=(
            jax.ShapeDtypeStruct(q_t.shape, F32),
            jax.ShapeDtypeStruct((own, 8, 2 * BLK), F32),
        ),
        in_specs=[smem(), smem(), smem(), vmem(), vmem(), vmem(), vmem()],
        out_specs=(vmem(), vmem()),
        scratch_shapes=[
            pltpu.VMEM((PAIRS, BLK, 2 * BLK), BF16),
            pltpu.VMEM((D, BLK), F32),
            pltpu.VMEM((8, 2 * BLK), F32),
            pltpu.VMEM((8, 2 * BLK), F32),
            pltpu.SMEM((ext,), jnp.int32),
            pltpu.SMEM((ext,), jnp.int32),
        ],
        compiler_params=pltpu.CompilerParams(vmem_limit_bytes=40 * 2**20),
        cost_estimate=cost(13),
        name="attend",
    )(flags, keep, pos, factor, q_t, k, v_t)


def backward_kernel(
    flags,
    keep,
    pos,
    log_factor,
    inv_factor,
    q_t,
    q,
    dc_t,
    dc,
    ctx_t,
    lse,
    k,
    k_t,
    v,
    dq_t,
    dk,
    dv,
    dr,
    qbd,
    cbd,
    q2,
    c2,
    dq_acc,
    dk_acc,
    dv_acc,
    delta,
    first_s,
    last_s,
    kept_s,
):
    own = q_t.shape[1] // BLK
    scan_blocks(flags, pos[0], first_s, last_s, own)
    qbd[...] = jnp.zeros_like(qbd)
    cbd[...] = jnp.zeros_like(cbd)
    dk_acc[...] = jnp.zeros_like(dk_acc)
    dv_acc[...] = jnp.zeros_like(dv_acc)
    dr[...] = jnp.zeros_like(dr)
    left = lax.broadcasted_iota(jnp.int32, (BLK, BLK), 1) < HD

    @pl.loop(0, own)
    def _(i):
        cols = pl.ds(pl.multiple_of(i * BLK, BLK), BLK)
        for hp in range(PAIRS):
            lanes = slice(hp * BLK, (hp + 1) * BLK)
            upper = pl.ds(hp * BLK, HD)
            lower = pl.ds(hp * BLK + HD, HD)
            qbd[hp, :HD, :BLK] = q_t[upper, cols]
            qbd[hp, HD:, BLK:] = q_t[lower, cols]
            cu = dc_t[upper, cols]
            cl = dc_t[lower, cols]
            cbd[hp, :HD, :BLK] = cu
            cbd[hp, HD:, BLK:] = cl
            delta[hp : hp + 1, :BLK] = jnp.sum(
                cu.astype(F32) * ctx_t[upper, cols], axis=0, keepdims=True
            )
            delta[hp : hp + 1, BLK:] = jnp.sum(
                cl.astype(F32) * ctx_t[lower, cols], axis=0, keepdims=True
            )
            qn = q[cols, lanes].astype(F32)
            cn = dc[cols, lanes].astype(F32)
            q2[hp, :BLK, :] = jnp.where(left, qn, 0.0).astype(BF16)
            q2[hp, BLK:, :] = jnp.where(left, 0.0, qn).astype(BF16)
            c2[hp, :BLK, :] = jnp.where(left, cn, 0.0).astype(BF16)
            c2[hp, BLK:, :] = jnp.where(left, 0.0, cn).astype(BF16)
        dq_acc[...] = jnp.zeros_like(dq_acc)
        me = i + RIM
        count = list_kept(keep, i, first_s, last_s, kept_s)

        @pl.loop(0, (count + 1) // 2)
        def _(n):
            ((rows_a, ab_a), (rows_b, ab_b)), void = two_kept(n, count, kept_s, first_s[me], me)
            for hp in range(PAIRS):
                lanes = slice(hp * BLK, (hp + 1) * BLK)
                one = slice(hp, hp + 1)
                vb = jnp.concatenate([v[rows_a, lanes], v[rows_b, lanes]], 0)
                s = dot(jnp.concatenate([k[rows_a, lanes], k[rows_b, lanes]], 0), qbd[hp])
                dw = dot(vb, cbd[hp])
                level = lse[i, one, :]
                w_a = jnp.exp2(s[:BLK] * SCALE2 + (log_factor[ab_a, one, :] - level))
                w_b = jnp.exp2(s[BLK:] * SCALE2 + (log_factor[ab_b, one, :] - level + void))
                ds_a = w_a * (dw[:BLK] - delta[one, :] * inv_factor[ab_a, one, :])
                ds_b = w_b * (dw[BLK:] - delta[one, :] * inv_factor[ab_b, one, :])
                wb = jnp.concatenate([w_a.astype(BF16), w_b.astype(BF16)], 0)
                dsb = jnp.concatenate([ds_a.astype(BF16), ds_b.astype(BF16)], 0)
                dvc = dot(wb, c2[hp])
                dkc = dot(dsb, q2[hp])
                dqc = dot(jnp.concatenate([k_t[lanes, rows_a], k_t[lanes, rows_b]], 1), dsb)
                dv_acc[rows_a, lanes] += dvc[:BLK]
                dv_acc[rows_b, lanes] += dvc[BLK:]
                dk_acc[rows_a, lanes] += dkc[:BLK]
                dk_acc[rows_b, lanes] += dkc[BLK:]
                upper = slice(hp * BLK, hp * BLK + HD)
                lower = slice(hp * BLK + HD, (hp + 1) * BLK)
                dq_acc[upper, :] += dqc[:HD, :BLK]
                dq_acc[lower, :] += dqc[HD:, BLK:]
                dots = dvc * vb.astype(F32)
                dr[ab_a, one, :] += jnp.sum(dots[:BLK], axis=0, keepdims=True)
                dr[ab_b, one, :] += jnp.sum(dots[BLK:], axis=0, keepdims=True)

        dq_t[:, cols] = (dq_acc[...] * SCALE).astype(BF16)

    ext = dk.shape[0] // BLK

    @pl.loop(0, ext)
    def _(e):
        rows = pl.ds(pl.multiple_of(e * BLK, BLK), BLK)
        dk[rows, :] = (dk_acc[rows, :] * SCALE).astype(BF16)
        dv[rows, :] = dv_acc[rows, :].astype(BF16)


def attend_back(flags, keep, pos, log_factor, inv_factor, q_t, q, dc_t, dc, ctx_t, lse, k, k_t, v):
    own = q_t.shape[1] // BLK
    ext = own + 2 * RIM
    return pl.pallas_call(
        backward_kernel,
        out_shape=(
            jax.ShapeDtypeStruct(q_t.shape, BF16),
            jax.ShapeDtypeStruct(k.shape, BF16),
            jax.ShapeDtypeStruct(v.shape, BF16),
            jax.ShapeDtypeStruct((SPAN * SPAN, 8, BLK), F32),
        ),
        in_specs=[smem()] * 3 + [vmem()] * 11,
        out_specs=(vmem(),) * 4,
        scratch_shapes=[
            pltpu.VMEM((PAIRS, BLK, 2 * BLK), BF16),
            pltpu.VMEM((PAIRS, BLK, 2 * BLK), BF16),
            pltpu.VMEM((PAIRS, 2 * BLK, BLK), BF16),
            pltpu.VMEM((PAIRS, 2 * BLK, BLK), BF16),
            pltpu.VMEM((D, BLK), F32),
            pltpu.VMEM((ext * BLK, D), F32),
            pltpu.VMEM((ext * BLK, D), F32),
            pltpu.VMEM((8, 2 * BLK), F32),
            pltpu.SMEM((ext,), jnp.int32),
            pltpu.SMEM((ext,), jnp.int32),
            pltpu.SMEM((ext,), jnp.int32),
        ],
        compiler_params=pltpu.CompilerParams(vmem_limit_bytes=56 * 2**20),
        cost_estimate=cost(5),
        name="attend_back",
    )(flags, keep, pos, log_factor, inv_factor, q_t, q, dc_t, dc, ctx_t, lse, k, k_t, v)


def centred_rows(x):
    middle = jnp.mean(x, -1, keepdims=True)
    c = x - middle
    spread = jnp.mean(c * c, -1, keepdims=True)
    r = lax.rsqrt(spread + 1e-06)
    return c * r, r

def gelu_and_slope(v):
    e = jnp.exp2(v * v * (-0.5 * math.log2(math.e)))
    t = 1.0 / (1.0 + jnp.abs(v) * (0.3275911 * math.sqrt(0.5)))
    q = t * (0.127414796 + t * (-0.142248368 + t * (0.7107068705 + t * (-0.7265760135 + t * 0.5307027145)))) * e
    phi = jnp.where(v >= 0, 1.0 - q, q)
    return v * phi, phi + v * (e * (1.0 / math.sqrt(2.0 * math.pi)))

ROWS = 256

def ffn_kernel(ctx_t, hidden, wo, w1, w2, vec, b1, first, normed_low, active, slope, second, result, result_low):
    x = hidden[...].astype(F32) + dot_rows(ctx_t[...].astype(BF16), wo[...]) + vec[0:1, :]
    first[...] = x
    hat, _ = centred_rows(x)
    normed = hat * vec[1:2, :] + vec[2:3, :]
    low = normed.astype(BF16)
    normed_low[...] = low
    total = normed + vec[3:4, :]
    for j in range(FF // D):
        cols = slice(j * D, (j + 1) * D)
        inner = dot(low, w1[:, cols]) + b1[:, cols]
        a, s = gelu_and_slope(inner)
        a = a.astype(BF16)
        active[:, cols] = a
        slope[:, cols] = s.astype(BF16)
        total = total + dot(a, w2[:, cols])
    second[...] = total
    hat, _ = centred_rows(total)
    x = hat * vec[4:5, :] + vec[5:6, :]
    result[...] = x
    result_low[...] = x.astype(BF16)

def ffn(ctx_t, hidden, wo, wo_at, w12, vec, b1):
    n = hidden.shape[0]
    row = lambda w: pl.BlockSpec((ROWS, w), lambda i: (i, 0))
    return pl.pallas_call(
        ffn_kernel,
        grid=(n // ROWS,),
        in_specs=[pl.BlockSpec((D, ROWS), lambda i: (0, i)), row(D), once((D, D), wo_at), once((D, FF)), once((D, FF), 1), once((8, D)), once((1, FF))],
        out_specs=[row(D), row(D), row(FF), row(FF), row(D), row(D), row(D)],
        out_shape=[jax.ShapeDtypeStruct((n, D), F32), jax.ShapeDtypeStruct((n, D), BF16), jax.ShapeDtypeStruct((n, FF), BF16),
                   jax.ShapeDtypeStruct((n, FF), BF16), jax.ShapeDtypeStruct((n, D), F32), jax.ShapeDtypeStruct((n, D), F32), jax.ShapeDtypeStruct((n, D), BF16)],
        compiler_params=pltpu.CompilerParams(vmem_limit_bytes=56 * 2**20),
        cost_estimate=cost(28),
        name="ffn",
    )(ctx_t, hidden, wo, w12, w12, vec, b1)

def ffn_back_kernel(grad, second, first, slope, w1, w2, wo, gains, douter, dinner, dfirst, dattend, dc, dc_t, sums, b1_sum):
    @pl.when(pl.program_id(0) == 0)
    def _():
        sums[...] = jnp.zeros_like(sums)
        b1_sum[...] = jnp.zeros_like(b1_sum)
    def back(g, x, gain):
        hat, r = centred_rows(x)
        e = g * gain
        return (e - jnp.mean(e, -1, keepdims=True) - hat * jnp.mean(e * hat, -1, keepdims=True)) * r, hat
    def column(v):
        return jnp.sum(v, 0, keepdims=True)
    g = grad[...].astype(F32)
    dsecond, hat = back(g, second[...], gains[4:5, :])
    sums[0:1, :] += column(g * hat)
    sums[1:2, :] += column(g)
    low = dsecond.astype(BF16)
    douter[...] = low
    sums[2:3, :] += column(low.astype(F32))
    dnormed = dsecond
    for j in range(FF // D):
        cols = slice(j * D, (j + 1) * D)
        d = (dot_cols(low, w2[:, cols]) * slope[:, cols].astype(F32)).astype(BF16)
        dinner[:, cols] = d
        b1_sum[:, cols] += column(d.astype(F32))
        dnormed = dnormed + dot_cols(d, w1[:, cols])
    dx, hat = back(dnormed, first[...], gains[1:2, :])
    sums[3:4, :] += column(dnormed * hat)
    sums[4:5, :] += column(dnormed)
    dfirst[...] = dx
    low = dx.astype(BF16)
    dattend[...] = low
    sums[5:6, :] += column(low.astype(F32))
    dc[...] = dot_cols(low, wo[...]).astype(BF16)
    dc_t[...] = dot_cols(wo[...], low).astype(BF16)

def ffn_back(grad, second, first, slope, w12, wo, wo_at, gains):
    n = grad.shape[0]
    row = lambda w: pl.BlockSpec((ROWS, w), lambda i: (i, 0))
    return pl.pallas_call(
        ffn_back_kernel,
        grid=(n // ROWS,),
        in_specs=[row(D), row(D), row(D), row(FF), once((D, FF)), once((D, FF), 1), once((D, D), wo_at), once((8, D))],
        out_specs=[row(D), row(FF), row(D), row(D), row(D), pl.BlockSpec((D, ROWS), lambda i: (0, i)), pl.BlockSpec((8, D), lambda i: (0, 0)), pl.BlockSpec((1, FF), lambda i: (0, 0))],
        out_shape=[jax.ShapeDtypeStruct((n, D), BF16), jax.ShapeDtypeStruct((n, FF), BF16), jax.ShapeDtypeStruct((n, D), F32),
                   jax.ShapeDtypeStruct((n, D), BF16), jax.ShapeDtypeStruct((n, D), BF16), jax.ShapeDtypeStruct((D, n), BF16),
                   jax.ShapeDtypeStruct((8, D), F32), jax.ShapeDtypeStruct((1, FF), F32)],
        compiler_params=pltpu.CompilerParams(vmem_limit_bytes=56 * 2**20),
        cost_estimate=cost(3),
        name="ffn_back",
    )(grad, second, first, slope, w12, w12, wo, gains)

def ffn_grads_kernel(extra, normed, dinner, active, douter, ctx_t, dattend, sums, b1_sum, *rest):
    (other, other_vec, out, turned) = rest if extra else (None, None) + rest
    n = pl.program_id(0)
    blocks = FF // D
    last = 2 * blocks + 1 + extra

    @pl.when(n == 0)
    def _():
        turned[...] = normed[...].T

    @pl.when(n < blocks)
    def _():
        out[...] = dot(turned[...], dinner[...]).astype(BF16)

    @pl.when(jnp.logical_and(n >= blocks, n < 2 * blocks))
    def _():
        out[...] = dot_rows(active[...], douter[...]).astype(BF16)

    @pl.when(n == 2 * blocks)
    def _():
        out[...] = dot(ctx_t[...].astype(BF16), dattend[...]).astype(BF16)

    @pl.when(n == last)
    def _():
        rows = [sums[...]] + [b1_sum[:, j * D : (j + 1) * D] for j in range(blocks)]
        rows = jnp.concatenate(rows + [jnp.zeros((BLK - 8 - blocks, D), F32)], 0)
        out[:, :BLK] = rows.T.astype(BF16)
        if extra:
            out[:, BLK : 2 * BLK] = other_vec[...]

    if extra:

        @pl.when(jnp.logical_and(n > 2 * blocks, n < last))
        def _():
            out[...] = other[...]


def ffn_grads(normed, dinner, active, douter, ctx_t, dattend, sums, b1_sum, other=None):
    n = normed.shape[0]
    blocks = FF // D
    extra = 0 if other is None else 3
    width = (2 * blocks + 1 + extra) * D + (2 if extra else 1) * BLK
    part = lambda first, count: (lambda i: (0, jnp.clip(i - first, 0, count - 1)))
    specs = [
        once((n, D)),
        pl.BlockSpec((n, D), part(0, blocks)),
        pl.BlockSpec((n, D), part(blocks, blocks)),
        once((n, D)),
        once((D, n)),
        once((n, D)),
        once((8, D)),
        once((1, FF)),
    ]
    args = [normed, dinner, active, douter, ctx_t, dattend, sums, b1_sum]
    if extra:
        specs += [pl.BlockSpec((D, D), part(2 * blocks + 1, extra)), once((D, BLK), extra * D // BLK)]
        args += [other, other]
    return pl.pallas_call(
        functools.partial(ffn_grads_kernel, extra),
        grid=(2 * blocks + 2 + extra,),
        in_specs=specs,
        out_specs=pl.BlockSpec((D, D), lambda i: (0, i)),
        out_shape=jax.ShapeDtypeStruct((D, width), BF16),
        scratch_shapes=[pltpu.VMEM((D, n), BF16)],
        compiler_params=pltpu.CompilerParams(vmem_limit_bytes=56 * 2**20),
        cost_estimate=cost(3),
        name="ffn_grads",
    )(*args)


def project_kernel(low, w, qb, vb, q, q_t, k, k_t, v, v_t):
    i = pl.program_id(0)
    n = pl.num_programs(0)
    x = low[...]
    kk = dot(x, w[:, D : 2 * D]).astype(BF16)
    k[...] = kk
    k_t[...] = kk.T
    vv = (dot(x, w[:, 2 * D : 3 * D]) + vb[...]).astype(BF16)
    v[...] = vv
    v_t[...] = vv.T
    skip = RIM * BLK // ROWS

    @pl.when(jnp.logical_and(i >= skip, i < n - skip))
    def _():
        qq = (dot(x, w[:, :D]) + qb[...]).astype(BF16)
        q[...] = qq
        q_t[...] = qq.T

def project(low_ext, w, qb, vb):
    n = low_ext.shape[0]
    rim = RIM * BLK
    skip = rim // ROWS
    own = n - 2 * rim
    last = own // ROWS - 1
    row = pl.BlockSpec((ROWS, D), lambda i: (i, 0))
    col = pl.BlockSpec((D, ROWS), lambda i: (0, i))
    qrow = pl.BlockSpec((ROWS, D), lambda i: (jnp.clip(i - skip, 0, last), 0))
    qcol = pl.BlockSpec((D, ROWS), lambda i: (0, jnp.clip(i - skip, 0, last)))
    tall = jax.ShapeDtypeStruct((n, D), BF16)
    wide = jax.ShapeDtypeStruct((D, n), BF16)
    return pl.pallas_call(
        project_kernel,
        grid=(n // ROWS,),
        in_specs=[row, once((D, 3 * D)), once((1, D)), once((1, D))],
        out_specs=[qrow, qcol, row, col, row, col],
        out_shape=[jax.ShapeDtypeStruct((own, D), BF16), jax.ShapeDtypeStruct((D, own), BF16), tall, wide, tall, wide],
        compiler_params=pltpu.CompilerParams(vmem_limit_bytes=40 * 2**20),
        cost_estimate=cost(14),
        name="project",
    )(low_ext, w, qb, vb)

def att_grads_kernel(low, dq_t, dk, dv, dr, rate, out, turned):
    n = pl.program_id(0)
    own = dq_t.shape[1]
    rim = (low.shape[0] - own) // 2

    @pl.when(n == 0)
    def _():
        turned[...] = low[...].T
        out[...] = dot_cols(turned[:, rim : rim + own], dq_t[...]).astype(BF16)

    @pl.when(n == 1)
    def _():
        out[...] = dot(turned[...], dk[...]).astype(BF16)

    @pl.when(n == 2)
    def _():
        out[...] = dot(turned[...], dv[...]).astype(BF16)

    @pl.when(n == 3)
    def _():
        qb = jnp.sum(dq_t[...].astype(F32), 1, keepdims=True)
        vb = jnp.sum(dv[...].astype(F32), 0, keepdims=True)
        left = lax.broadcasted_iota(jnp.int32, (SPAN * SPAN, BLK), 1) < HD
        columns = []
        for hp in range(PAIRS):
            both = dr[:, hp, :]
            columns.append(jnp.sum(jnp.where(left, both, 0.0), 1, keepdims=True))
            columns.append(jnp.sum(jnp.where(left, 0.0, both), 1, keepdims=True))
        logit = jnp.concatenate(columns, 0) * rate[...]
        rows = jnp.concatenate([vb, jnp.zeros((127, D), F32)], 0).T
        lane = lax.broadcasted_iota(jnp.int32, (D, 128), 1)
        out[:, :128] = jnp.where(lane == 2, qb, jnp.where(lane == 1, logit, rows)).astype(BF16)

def att_grads(low_ext, dq_t, dk, dv, dr, rate):
    n = low_ext.shape[0]
    own = dq_t.shape[1]
    return pl.pallas_call(
        att_grads_kernel,
        grid=(4,),
        in_specs=[once((n, D)), once((D, own)), once((n, D)), once((n, D)), once(dr.shape), once((D, 1))],
        out_specs=pl.BlockSpec((D, D), lambda i: (0, i)),
        out_shape=jax.ShapeDtypeStruct((D, 3 * D + 128), BF16),
        scratch_shapes=[pltpu.VMEM((D, n), BF16)],
        compiler_params=pltpu.CompilerParams(vmem_limit_bytes=48 * 2**20),
        cost_estimate=cost(3),
        name="att_grads",
    )(low_ext, dq_t, dk, dv, dr, rate)

def input_back_kernel(dk, dv, dq_t, dfirst, w, own, rims):
    i = pl.program_id(0)
    n = pl.num_programs(0)
    skip = RIM * BLK // ROWS
    total = dot_cols(dk[...], w[:, D : 2 * D]) + dot_cols(dv[...], w[:, 2 * D : 3 * D])
    inside = jnp.logical_and(i >= skip, i < n - skip)

    @pl.when(inside)
    def _():
        own[...] = total + dot_tt(dq_t[...], w[:, :D]) + dfirst[...]

    @pl.when(jnp.logical_not(inside))
    def _():
        rims[...] = total.astype(BF16)

def input_back(dk, dv, dq_t, dfirst, w):
    n = dk.shape[0]
    own = dfirst.shape[0]
    skip = (n - own) // 2 // ROWS
    last = own // ROWS - 1
    row = pl.BlockSpec((ROWS, D), lambda i: (i, 0))
    orow = pl.BlockSpec((ROWS, D), lambda i: (jnp.clip(i - skip, 0, last), 0))
    ocol = pl.BlockSpec((D, ROWS), lambda i: (0, jnp.clip(i - skip, 0, last)))
    rrow = pl.BlockSpec((ROWS, D), lambda i: (jnp.where(i < skip, i, jnp.maximum(i - last - 1, skip)), 0))
    return pl.pallas_call(
        input_back_kernel,
        grid=(n // ROWS,),
        in_specs=[row, row, ocol, orow, once((D, 3 * D))],
        out_specs=[orow, rrow],
        out_shape=[jax.ShapeDtypeStruct((own, D), F32), jax.ShapeDtypeStruct((n - own, D), BF16)],
        compiler_params=pltpu.CompilerParams(vmem_limit_bytes=40 * 2**20),
        cost_estimate=cost(3),
        name="input_back",
    )(dk, dv, dq_t, dfirst, w)


def neighbours(tail, head):
    count = lax.axis_size("dp")
    return (
        lax.ppermute(tail, "dp", [(i, i + 1) for i in range(count - 1)]),
        lax.ppermute(head, "dp", [(i + 1, i) for i in range(count - 1)]),
    )


def gathered(part):
    return lax.all_gather(part, AXES, axis=0, tiled=True)


def place():
    dp = lax.axis_index("dp")
    mp = lax.axis_index("mp")
    return dp // 2, (dp % 2) * (lax.axis_size("mp") // 2) + mp // 2, mp % 2


def sizes():
    return lax.axis_size("dp") // 2, lax.axis_size("mp")


def swap(block, mask):
    count = lax.axis_size("dp") * lax.axis_size("mp")
    return lax.ppermute(block, AXES, [(i, i ^ mask) for i in range(count)])


def put(buffer, piece, index):
    return lax.dynamic_update_slice(buffer, piece[None], (index,) + (0,) * piece.ndim)


class SteppedGather:
    def __init__(self, part):
        self.part = part
        self.block = part
        self.step = 0

    def settle(self, tied):
        if self.step > 0:
            own = place()[self.step - 1]
            out = jnp.zeros((len(self.arriving) + 1,) + self.block.shape, self.block.dtype)
            tied, out = lax.optimization_barrier((tied, out))
            out = put(out, self.block, own)
            for d, piece in self.arriving:
                out = put(out, piece, own ^ d)
            self.block = out
        return tied

    def advance(self, tied):
        far, middle = sizes()
        tied = self.settle(tied)
        tied, self.block = lax.optimization_barrier((tied, self.block))
        self.step += 1
        count, scale = ((far, 2 * middle), (middle, 2), (2, 1))[self.step - 1]
        self.arriving = [(d, swap(self.block, d * scale)) for d in range(1, count)]
        return tied

    def result(self, tied):
        self.settle(tied)
        return self.block.transpose(2, 1, 0, 3, 4).reshape(-1, self.part.shape[1])


def scattered(part):
    return lax.psum_scatter(part, AXES, scatter_dimension=0, tiled=True).astype(F32)


def pick(array, index, axis):
    return lax.dynamic_index_in_dim(array, index, axis, keepdims=False)


class SteppedSum:
    def __init__(self, part):
        far, middle = sizes()
        self.parts = part.reshape(far, middle, 2, -1, part.shape[1])
        self.step = 0

    def anchored(self, tied):
        tied, kept = lax.optimization_barrier((tied, self.halves[0]))
        return tied, (kept, self.halves[1])

    def middle_sum(self, index):
        kept, got = self.halves
        return pick(kept, index, 1).astype(F32) + pick(got, index, 1).astype(F32)

    def far_sum(self, index):
        z, m, c = place()
        total = self.middle_own(index)
        for piece in self.arrived:
            total = total + pick(piece, index, 0).astype(F32)
        return total

    def middle_own(self, index):
        z, m, c = place()
        kept, got = self.halves
        return pick(pick(kept, m, 1), index, 0).astype(F32) + pick(
            pick(got, m, 1), index, 0
        ).astype(F32)

    def advance(self, tied):
        far, middle = sizes()
        z, m, c = place()
        self.step += 1
        if self.step == 1:
            out = pick(self.parts, 1 - c, 2)
            tied, out = lax.optimization_barrier((tied, out))
            self.halves = (pick(self.parts, c, 2), swap(out, 1))
        elif self.step == 2:
            tied, self.halves = self.anchored(tied)
            out = [self.middle_sum(m ^ d).astype(BF16) for d in range(1, middle)]
            tied, out = lax.optimization_barrier((tied, out))
            self.arrived = [swap(item, d * 2) for d, item in zip(range(1, middle), out)]
        else:
            tied, self.halves = self.anchored(tied)
            out = [self.far_sum(z ^ d).astype(BF16) for d in range(1, far)]
            tied, out = lax.optimization_barrier((tied, out))
            self.last = [swap(item, d * 2 * middle) for d, item in zip(range(1, far), out)]
        return tied

    def result(self):
        z, m, c = place()
        total = self.far_sum(z)
        for piece in self.last:
            total = total + piece.astype(F32)
        return total


def table_rows(table):
    rows = table.reshape(PAIRS, 2, SPAN * SPAN).transpose(2, 0, 1)
    return jnp.repeat(rows, BLK, axis=2)


def layer_forward(hidden, low_ext, head, vec, flags, keep, temper, pos, between):
    z = (vec["logits"] + vec["jitter"]).reshape(HEADS, SPAN, SPAN) / temper[:, None, None]
    relaxed = jax.nn.sigmoid(z)
    factor = table_rows(relaxed)
    q, q_t, k, k_t, v, v_t = project(low_ext, head, vec["qb"][None], vec["vb"][None])
    log_factor, inv_factor = jnp.log2(factor), 1.0 / factor
    ctx_t, lse = attend(flags, keep, pos, factor, q_t, k, v_t)
    ctx_t, wo, wo_at, w12 = between(ctx_t)
    names = ("ob", "g1", "s1", "b2", "g2", "s2", "s2", "s2")
    vectors = jnp.stack([vec[name] for name in names])
    first, normed_low, active, slope, second, result, result_low = ffn(
        ctx_t, hidden, wo, wo_at, w12, vectors, vec["b1"][None]
    )
    record = (low_ext, q, q_t, k, k_t, v, ctx_t, lse, first, normed_low, active, slope, second)
    return result, result_low, record + (relaxed, log_factor, inv_factor, vectors, head, wo, wo_at, w12)


def layer_backward(grad, record, flags, keep, temper, pos, before=None, done=None):
    low_ext, q, q_t, k, k_t, v, ctx_t, lse, first, normed_low, active, slope, second = record[:13]
    relaxed, log_factor, inv_factor, vectors, head, wo, wo_at, w12 = record[13:]
    rows = first.shape[0]
    rim = RIM * BLK
    douter, dinner, dfirst, dattend, dc, dc_t, row_sums, b1_sum = ffn_back(
        grad, second, first, slope, w12, wo, wo_at, vectors
    )
    part = ffn_grads(normed_low, dinner, active, douter, ctx_t, dattend, row_sums, b1_sum, before)
    if before is None:
        dc, part = lax.optimization_barrier((dc, part))
        ffn_sum = scattered(part)
    else:
        ffn_sum = SteppedSum(part)
        dc = ffn_sum.advance(dc)
        dc = ffn_sum.advance(dc)
    dq_t, dk, dv, dr = attend_back(
        flags, keep, pos, log_factor, inv_factor, q_t, q, dc_t, dc, ctx_t, lse, k, k_t, v
    )
    rate = ((1.0 - relaxed) / temper[:, None, None]).reshape(-1, 1)
    if before is None:
        own, rims = input_back(dk, dv, dq_t, dfirst, head)
        from_lower, from_upper = neighbours(rims[rim:], rims[:rim])
        dq_t, rims = lax.optimization_barrier((dq_t, rims))
        att_sum = att_grads(low_ext, dq_t, dk, dv, dr, rate)
    else:
        att_sum = SteppedSum(att_grads(low_ext, dq_t, dk, dv, dr, rate))
        dk = att_sum.advance(dk)
        dk, done = lax.optimization_barrier((dk, done))
        dk = ffn_sum.advance(dk)
        own, rims = input_back(dk, dv, dq_t, dfirst, head)
        own = att_sum.advance(own)
        from_lower, from_upper = neighbours(rims[rim:], rims[:rim])
        own = att_sum.advance(own)
    dhidden = own.at[:rim].add(from_lower.astype(F32))
    dhidden = dhidden.at[rows - rim :].add(from_upper.astype(F32))
    return dhidden, ffn_sum, att_sum, done


def per_device(
    embedded,
    opening,
    selector,
    wq,
    wk,
    wv,
    wo,
    qb,
    vb,
    ob,
    g1,
    s1,
    w1,
    b1,
    w2,
    b2,
    g2,
    s2,
    scores,
    jitter,
    warmth,
    upstream,
):
    share = wq.shape[1]
    devices = D // share
    flags = opening[0]
    pos = lax.axis_index("dp").reshape(1).astype(jnp.int32)
    rim = RIM * BLK

    def widened(part):
        lead = part.shape[:-1]
        return jnp.swapaxes(part.reshape(lead + (devices, 4, share)), -3, -2).reshape(lead + (FF,))

    def unwidened(part):
        lead = part.shape[:-1]
        return jnp.swapaxes(part.reshape(lead + (4, devices, share)), -3, -2).reshape(lead + (FF,))

    def own_parts(tier):
        narrow = w2[tier].reshape(4, share, D)
        vectors = jnp.stack(
            [item[tier] for item in (qb, vb, ob, g1, s1, b2, g2, s2, scores, jitter)]
            + [b1[tier].reshape(4, share)[j] for j in range(4)],
            1,
        )
        vectors = jnp.pad(vectors, ((0, 0), (0, 128 - vectors.shape[1])))
        first = [wq[tier], wk[tier], wv[tier]]
        wide = [widened(w1[tier])] + [narrow[j] for j in range(4)]
        return first, wide, [wo[tier]], [vectors]

    def unpacked(columns):
        columns = jnp.transpose(columns.astype(F32))
        names = ("qb", "vb", "ob", "g1", "s1", "b2", "g2", "s2", "logits", "jitter")
        vec = {name: columns[n] for n, name in enumerate(names)}
        vec["b1"] = columns[len(names) : len(names) + 4].reshape(FF)
        return vec

    symbols = embedded[0]
    first, wide, out, vectors = own_parts(0)
    gather = SteppedGather(jnp.concatenate(first + vectors, 1))
    for _ in range(3):
        symbols = gather.advance(symbols)
    lower, upper = neighbours(symbols[symbols.shape[0] - rim :], symbols[:rim])
    low_ext = jnp.concatenate([lower, symbols, upper], 0)
    head_zero = gather.result(symbols)
    head_zero, *rest = lax.optimization_barrier((head_zero, *wide, *out))
    tail_zero = gathered(jnp.concatenate(rest, 1))
    first, wide, out, vectors = own_parts(1)
    later = SteppedGather(jnp.concatenate(first + out + vectors, 1))
    tails = []

    def between_zero(ctx_t):
        ctx_t = later.advance(ctx_t)
        ctx_t = later.advance(ctx_t)
        _, _, *rest = lax.optimization_barrier((ctx_t, tail_zero, *wide))
        tails.append(gathered(jnp.concatenate(rest, 1)))
        return ctx_t, tail_zero, 2 * FF // D, tail_zero

    def between_one(ctx_t):
        return ctx_t, head_one, 3, tails[0]

    hidden, low, record = layer_forward(
        symbols,
        low_ext,
        head_zero,
        unpacked(head_zero[:, 3 * D :]),
        flags,
        selector[0, 0],
        warmth[0],
        pos,
        between_zero,
    )
    records = [record]
    low = later.advance(low)
    lower, upper = neighbours(low[low.shape[0] - rim :], low[:rim])
    low_ext = jnp.concatenate([lower, low, upper], 0)
    head_one = later.result(low)
    hidden, _, record = layer_forward(
        hidden,
        low_ext,
        head_one,
        unpacked(head_one[:, 4 * D :]),
        flags,
        selector[1, 0],
        warmth[1],
        pos,
        between_one,
    )
    records.append(record)
    grad = upstream[0]
    grad, ffn_one, att_one, _ = layer_backward(
        grad, records[1], flags, selector[1, 0], warmth[1], pos
    )
    grad, ffn_zero, att_zero, ffn_one = layer_backward(
        grad, records[0], flags, selector[0, 0], warmth[0], pos, att_one, ffn_one
    )
    both = ffn_zero.result()
    last = att_zero.result()
    ends = [2 * FF + D, 2 * FF + 4 * D]
    fv = jnp.stack([both[:, ends[1] : ends[1] + BLK], ffn_one[:, ends[0] :]])
    av = jnp.stack([last[:, 3 * D :], both[:, ends[1] + BLK :]])
    ffn_sums = jnp.stack([both[:, : ends[0]], ffn_one[:, : ends[0]]])
    att = jnp.stack([last[:, : 3 * D], both[:, ends[0] : ends[1]]])
    w1_grad = unwidened(ffn_sums[:, :, :FF])
    w2_grad = jnp.concatenate([ffn_sums[:, :, FF + j * D : FF + (j + 1) * D] for j in range(4)], 1)
    wo_grad = ffn_sums[:, :, 2 * FF :]
    b1_grad = jnp.concatenate([fv[:, :, 8 + j] for j in range(4)], 1)
    new_mask = (scores.astype(F32) + jitter.astype(F32) > 0).astype(jnp.int32)
    return (
        hidden[None],
        grad[None],
        att[:, :, :D],
        att[:, :, D : 2 * D],
        att[:, :, 2 * D : 3 * D],
        wo_grad,
        av[:, :, 2],
        av[:, :, 0],
        fv[:, :, 5],
        fv[:, :, 3],
        fv[:, :, 4],
        w1_grad,
        b1_grad,
        w2_grad,
        fv[:, :, 2],
        fv[:, :, 0],
        fv[:, :, 1],
        av[:, :, 1],
        new_mask,
    )


def solution(mesh):
    rows = P("mp", "dp", None)
    matrix = P(None, AXES, None)
    vector = P(None, AXES)
    return jax.shard_map(
        per_device,
        mesh=mesh,
        in_specs=(rows, P("mp", None), P(None, "mp", "dp", None))
        + (matrix,) * 4
        + (vector,) * 5
        + (matrix, vector, matrix)
        + (vector,) * 5
        + (P(), rows),
        out_specs=(rows, rows)
        + (matrix,) * 4
        + (vector,) * 5
        + (matrix, vector, matrix)
        + (vector,) * 5,
        check_vma=False,
    )
```

```python
import functools
import math

import jax
import jax.numpy as jnp
from jax import lax
from jax.experimental import pallas as pl
from jax.experimental.pallas import tpu as pltpu
from jax.sharding import PartitionSpec as P

D = 768
HEADS = 12
HD = 64
FF = 3072
BLK = 128
SPAN = 8
RIM = 4
PAIRS = HEADS // 2
AXES = ("dp", "mp")
SCALE = HD**-0.5
SCALE2 = SCALE * math.log2(math.e)
F32 = jnp.float32
BF16 = jnp.bfloat16


def cost(us):
    return pl.CostEstimate(flops=int(us * 1e9), bytes_accessed=1_000_000, transcendentals=0)


def once(shape, column=0):
    return pl.BlockSpec(shape, lambda i: (0,) * (len(shape) - 1) + (column,), pipeline_mode=pl.Buffered(1))


def dot(a, b):
    return jnp.dot(a, b, preferred_element_type=F32)


def dot_rows(a, b):
    return lax.dot_general(a, b, (((0,), (0,)), ((), ())), preferred_element_type=F32)


def dot_cols(a, b):
    return lax.dot_general(a, b, (((1,), (1,)), ((), ())), preferred_element_type=F32)


def dot_tt(a, b):
    return lax.dot_general(a, b, (((0,), (1,)), ((), ())), preferred_element_type=F32)


def scan_blocks(flags, pos, first_s, last_s, own):
    ext = own + 2 * RIM
    total = flags.shape[0]
    base = pos * own - RIM

    def opens(e):
        gid = base + e
        inside = jnp.logical_and(gid >= 0, gid < total)
        return jnp.where(inside, flags[jnp.clip(gid, 0, total - 1)], 1)

    def up(e, start):
        start = jnp.where(opens(e) == 1, e, start)
        first_s[e] = start
        return start

    lax.fori_loop(0, ext, up, jnp.int32(0))

    def down(n, stop):
        e = ext - 1 - n
        last_s[e] = stop
        return jnp.where(opens(e) == 1, e, stop)

    lax.fori_loop(0, ext, down, jnp.int32(ext))


def list_kept(keep, i, first_s, last_s, kept_s):
    me = i + RIM

    def one(e, count):
        wanted = jnp.logical_or(e == me, keep[i, jnp.clip(e - me + SPAN - 1, 0, 2 * SPAN - 2)] > 0)

        @pl.when(wanted)
        def _():
            kept_s[count] = e

        return count + wanted.astype(jnp.int32)

    return lax.fori_loop(first_s[me], last_s[me], one, jnp.int32(0))


def two_kept(n, count, kept_s, start, me):
    out = []
    for e in (kept_s[2 * n], kept_s[jnp.minimum(2 * n + 1, count - 1)]):
        rows = pl.ds(pl.multiple_of(e * BLK, BLK), BLK)
        out.append((rows, (me - start) * SPAN + (e - start)))
    void = jnp.where(2 * n + 1 < count, 0.0, -1e30).astype(F32)
    return out, void


def forward_kernel(
    flags, keep, pos, factor, q_t, k, v_t, ctx_t, lse, qbd, acc, top, total, first_s, last_s
):
    own = q_t.shape[1] // BLK
    scan_blocks(flags, pos[0], first_s, last_s, own)
    qbd[...] = jnp.zeros_like(qbd)

    @pl.loop(0, own)
    def _(i):
        cols = pl.ds(pl.multiple_of(i * BLK, BLK), BLK)
        for hp in range(PAIRS):
            qbd[hp, :HD, :BLK] = q_t[pl.ds(hp * BLK, HD), cols]
            qbd[hp, HD:, BLK:] = q_t[pl.ds(hp * BLK + HD, HD), cols]
        acc[...] = jnp.zeros_like(acc)
        top[...] = jnp.full_like(top, -1e30)
        total[...] = jnp.zeros_like(total)
        me = i + RIM
        start = first_s[me]

        @pl.loop(start, last_s[me])
        def _(e):
            wanted = jnp.logical_or(e == me, keep[i, jnp.clip(e - me + SPAN - 1, 0, 2 * SPAN - 2)] > 0)

            @pl.when(wanted)
            def _():
                rows = pl.ds(pl.multiple_of(e * BLK, BLK), BLK)
                ab = (me - start) * SPAN + (e - start)
                for hp in range(PAIRS):
                    lanes = slice(hp * BLK, (hp + 1) * BLK)
                    s = dot(k[rows, lanes], qbd[hp])
                    m_old = top[hp : hp + 1, :]
                    m_new = jnp.maximum(m_old, jnp.max(s, axis=0, keepdims=True))
                    p = jnp.exp2((s - m_new) * SCALE2)
                    alpha = jnp.exp2((m_old - m_new) * SCALE2)
                    total[hp : hp + 1, :] = total[hp : hp + 1, :] * alpha + jnp.sum(
                        p, axis=0, keepdims=True
                    )
                    top[hp : hp + 1, :] = m_new
                    c = dot(v_t[lanes, rows], p.astype(BF16))
                    f = factor[ab, hp : hp + 1, :]
                    upper = slice(hp * BLK, hp * BLK + HD)
                    lower = slice(hp * BLK + HD, (hp + 1) * BLK)
                    acc[upper, :] = acc[upper, :] * alpha[:, :BLK] + c[:HD, :BLK] * f[:, :BLK]
                    acc[lower, :] = acc[lower, :] * alpha[:, BLK:] + c[HD:, BLK:] * f[:, BLK:]

        for hp in range(PAIRS):
            t = total[hp : hp + 1, :]
            r = 1.0 / t
            upper = slice(hp * BLK, hp * BLK + HD)
            lower = slice(hp * BLK + HD, (hp + 1) * BLK)
            ctx_t[upper, cols] = acc[upper, :] * r[:, :BLK]
            ctx_t[lower, cols] = acc[lower, :] * r[:, BLK:]
            lse[i, hp : hp + 1, :] = top[hp : hp + 1, :] * SCALE2 + jnp.log2(t)


def smem():
    return pl.BlockSpec(memory_space=pltpu.SMEM)


def vmem():
    return pl.BlockSpec(memory_space=pltpu.VMEM)


def unwiden_kernel(a, b, out):
    share = a.shape[0]
    for n, ref in enumerate((a, b)):
        for d in range(D // share):
            pieces = [ref[:, j * D + share * d : j * D + share * (d + 1)] for j in range(FF // D)]
            for j, piece in enumerate(pieces):
                at = FF // D * share * d + share * j
                out[n, :, at : at + share] = piece


def unwiden(a, b):
    share = a.shape[0]
    return pl.pallas_call(
        unwiden_kernel,
        grid=(1,),
        in_specs=[pl.BlockSpec((share, FF), lambda i: (0, 0))] * 2,
        out_specs=pl.BlockSpec((2, share, FF), lambda i: (0, 0, 0)),
        out_shape=jax.ShapeDtypeStruct((2, share, FF), F32),
        cost_estimate=cost(2),
        name="unwiden",
    )(a, b)


def attend(flags, keep, pos, factor, q_t, k, v_t):
    own = q_t.shape[1] // BLK
    ext = own + 2 * RIM
    return pl.pallas_call(
        forward_kernel,
        out_shape=(
            jax.ShapeDtypeStruct(q_t.shape, F32),
            jax.ShapeDtypeStruct((own, 8, 2 * BLK), F32),
        ),
        in_specs=[smem(), smem(), smem(), vmem(), vmem(), vmem(), vmem()],
        out_specs=(vmem(), vmem()),
        scratch_shapes=[
            pltpu.VMEM((PAIRS, BLK, 2 * BLK), BF16),
            pltpu.VMEM((D, BLK), F32),
            pltpu.VMEM((8, 2 * BLK), F32),
            pltpu.VMEM((8, 2 * BLK), F32),
            pltpu.SMEM((ext,), jnp.int32),
            pltpu.SMEM((ext,), jnp.int32),
        ],
        compiler_params=pltpu.CompilerParams(vmem_limit_bytes=40 * 2**20),
        cost_estimate=cost(13),
        name="attend",
    )(flags, keep, pos, factor, q_t, k, v_t)


def backward_kernel(
    flags,
    keep,
    pos,
    log_factor,
    inv_factor,
    q_t,
    q,
    dc_t,
    dc,
    ctx_t,
    lse,
    k,
    k_t,
    v,
    dq_t,
    dk,
    dv,
    dr,
    qbd,
    cbd,
    q2,
    c2,
    dq_acc,
    dk_acc,
    dv_acc,
    delta,
    first_s,
    last_s,
    kept_s,
):
    own = q_t.shape[1] // BLK
    scan_blocks(flags, pos[0], first_s, last_s, own)
    qbd[...] = jnp.zeros_like(qbd)
    cbd[...] = jnp.zeros_like(cbd)
    dk_acc[...] = jnp.zeros_like(dk_acc)
    dv_acc[...] = jnp.zeros_like(dv_acc)
    dr[...] = jnp.zeros_like(dr)
    left = lax.broadcasted_iota(jnp.int32, (BLK, BLK), 1) < HD

    @pl.loop(0, own)
    def _(i):
        cols = pl.ds(pl.multiple_of(i * BLK, BLK), BLK)
        for hp in range(PAIRS):
            lanes = slice(hp * BLK, (hp + 1) * BLK)
            upper = pl.ds(hp * BLK, HD)
            lower = pl.ds(hp * BLK + HD, HD)
            qbd[hp, :HD, :BLK] = q_t[upper, cols]
            qbd[hp, HD:, BLK:] = q_t[lower, cols]
            cu = dc_t[upper, cols]
            cl = dc_t[lower, cols]
            cbd[hp, :HD, :BLK] = cu
            cbd[hp, HD:, BLK:] = cl
            delta[hp : hp + 1, :BLK] = jnp.sum(
                cu.astype(F32) * ctx_t[upper, cols], axis=0, keepdims=True
            )
            delta[hp : hp + 1, BLK:] = jnp.sum(
                cl.astype(F32) * ctx_t[lower, cols], axis=0, keepdims=True
            )
            qn = q[cols, lanes].astype(F32)
            cn = dc[cols, lanes].astype(F32)
            q2[hp, :BLK, :] = jnp.where(left, qn, 0.0).astype(BF16)
            q2[hp, BLK:, :] = jnp.where(left, 0.0, qn).astype(BF16)
            c2[hp, :BLK, :] = jnp.where(left, cn, 0.0).astype(BF16)
            c2[hp, BLK:, :] = jnp.where(left, 0.0, cn).astype(BF16)
        dq_acc[...] = jnp.zeros_like(dq_acc)
        me = i + RIM
        count = list_kept(keep, i, first_s, last_s, kept_s)

        @pl.loop(0, (count + 1) // 2)
        def _(n):
            ((rows_a, ab_a), (rows_b, ab_b)), void = two_kept(n, count, kept_s, first_s[me], me)
            for hp in range(PAIRS):
                lanes = slice(hp * BLK, (hp + 1) * BLK)
                one = slice(hp, hp + 1)
                vb = jnp.concatenate([v[rows_a, lanes], v[rows_b, lanes]], 0)
                s = dot(jnp.concatenate([k[rows_a, lanes], k[rows_b, lanes]], 0), qbd[hp])
                dw = dot(vb, cbd[hp])
                level = lse[i, one, :]
                w_a = jnp.exp2(s[:BLK] * SCALE2 + (log_factor[ab_a, one, :] - level))
                w_b = jnp.exp2(s[BLK:] * SCALE2 + (log_factor[ab_b, one, :] - level + void))
                ds_a = w_a * (dw[:BLK] - delta[one, :] * inv_factor[ab_a, one, :])
                ds_b = w_b * (dw[BLK:] - delta[one, :] * inv_factor[ab_b, one, :])
                wb = jnp.concatenate([w_a.astype(BF16), w_b.astype(BF16)], 0)
                dsb = jnp.concatenate([ds_a.astype(BF16), ds_b.astype(BF16)], 0)
                dvc = dot(wb, c2[hp])
                dkc = dot(dsb, q2[hp])
                dqc = dot(jnp.concatenate([k_t[lanes, rows_a], k_t[lanes, rows_b]], 1), dsb)
                dv_acc[rows_a, lanes] += dvc[:BLK]
                dv_acc[rows_b, lanes] += dvc[BLK:]
                dk_acc[rows_a, lanes] += dkc[:BLK]
                dk_acc[rows_b, lanes] += dkc[BLK:]
                upper = slice(hp * BLK, hp * BLK + HD)
                lower = slice(hp * BLK + HD, (hp + 1) * BLK)
                dq_acc[upper, :] += dqc[:HD, :BLK]
                dq_acc[lower, :] += dqc[HD:, BLK:]
                dots = dvc * vb.astype(F32)
                dr[ab_a, one, :] += jnp.sum(dots[:BLK], axis=0, keepdims=True)
                dr[ab_b, one, :] += jnp.sum(dots[BLK:], axis=0, keepdims=True)

        dq_t[:, cols] = (dq_acc[...] * SCALE).astype(BF16)

    ext = dk.shape[0] // BLK

    @pl.loop(0, ext)
    def _(e):
        rows = pl.ds(pl.multiple_of(e * BLK, BLK), BLK)
        dk[rows, :] = (dk_acc[rows, :] * SCALE).astype(BF16)
        dv[rows, :] = dv_acc[rows, :].astype(BF16)


def attend_back(flags, keep, pos, log_factor, inv_factor, q_t, q, dc_t, dc, ctx_t, lse, k, k_t, v):
    own = q_t.shape[1] // BLK
    ext = own + 2 * RIM
    return pl.pallas_call(
        backward_kernel,
        out_shape=(
            jax.ShapeDtypeStruct(q_t.shape, BF16),
            jax.ShapeDtypeStruct(k.shape, BF16),
            jax.ShapeDtypeStruct(v.shape, BF16),
            jax.ShapeDtypeStruct((SPAN * SPAN, 8, BLK), F32),
        ),
        in_specs=[smem()] * 3 + [vmem()] * 11,
        out_specs=(vmem(),) * 4,
        scratch_shapes=[
            pltpu.VMEM((PAIRS, BLK, 2 * BLK), BF16),
            pltpu.VMEM((PAIRS, BLK, 2 * BLK), BF16),
            pltpu.VMEM((PAIRS, 2 * BLK, BLK), BF16),
            pltpu.VMEM((PAIRS, 2 * BLK, BLK), BF16),
            pltpu.VMEM((D, BLK), F32),
            pltpu.VMEM((ext * BLK, D), F32),
            pltpu.VMEM((ext * BLK, D), F32),
            pltpu.VMEM((8, 2 * BLK), F32),
            pltpu.SMEM((ext,), jnp.int32),
            pltpu.SMEM((ext,), jnp.int32),
            pltpu.SMEM((ext,), jnp.int32),
        ],
        compiler_params=pltpu.CompilerParams(vmem_limit_bytes=56 * 2**20),
        cost_estimate=cost(1),
        name="attend_back",
    )(flags, keep, pos, log_factor, inv_factor, q_t, q, dc_t, dc, ctx_t, lse, k, k_t, v)


def centred_rows(x):
    middle = jnp.mean(x, -1, keepdims=True)
    c = x - middle
    spread = jnp.mean(c * c, -1, keepdims=True)
    r = lax.rsqrt(spread + 1e-06)
    return c * r, r

def gelu_and_slope(v):
    e = jnp.exp2(v * v * (-0.5 * math.log2(math.e)))
    t = 1.0 / (1.0 + jnp.abs(v) * (0.3275911 * math.sqrt(0.5)))
    q = t * (0.127414796 + t * (-0.142248368 + t * (0.7107068705 + t * (-0.7265760135 + t * 0.5307027145)))) * e
    phi = jnp.where(v >= 0, 1.0 - q, q)
    return v * phi, phi + v * (e * (1.0 / math.sqrt(2.0 * math.pi)))

ROWS = 256

def ffn_kernel(ctx_t, hidden, wo, w1, w2, vec, b1, first, normed_low, active, slope, second, result, result_low):
    x = hidden[...].astype(F32) + dot_rows(ctx_t[...].astype(BF16), wo[...]) + vec[0:1, :]
    first[...] = x
    hat, _ = centred_rows(x)
    normed = hat * vec[1:2, :] + vec[2:3, :]
    low = normed.astype(BF16)
    normed_low[...] = low
    total = normed + vec[3:4, :]
    for j in range(FF // D):
        cols = slice(j * D, (j + 1) * D)
        inner = dot(low, w1[:, cols]) + b1[:, cols]
        a, s = gelu_and_slope(inner)
        a = a.astype(BF16)
        active[:, cols] = a
        slope[:, cols] = s.astype(BF16)
        total = total + dot(a, w2[:, cols])
    second[...] = total
    hat, _ = centred_rows(total)
    x = hat * vec[4:5, :] + vec[5:6, :]
    result[...] = x
    result_low[...] = x.astype(BF16)

def ffn(ctx_t, hidden, wo, wo_at, w12, vec, b1):
    n = hidden.shape[0]
    row = lambda w: pl.BlockSpec((ROWS, w), lambda i: (i, 0))
    return pl.pallas_call(
        ffn_kernel,
        grid=(n // ROWS,),
        in_specs=[pl.BlockSpec((D, ROWS), lambda i: (0, i)), row(D), once((D, D), wo_at), once((D, FF)), once((D, FF), 1), once((8, D)), once((1, FF))],
        out_specs=[row(D), row(D), row(FF), row(FF), row(D), row(D), row(D)],
        out_shape=[jax.ShapeDtypeStruct((n, D), F32), jax.ShapeDtypeStruct((n, D), BF16), jax.ShapeDtypeStruct((n, FF), BF16),
                   jax.ShapeDtypeStruct((n, FF), BF16), jax.ShapeDtypeStruct((n, D), F32), jax.ShapeDtypeStruct((n, D), F32), jax.ShapeDtypeStruct((n, D), BF16)],
        compiler_params=pltpu.CompilerParams(vmem_limit_bytes=56 * 2**20),
        cost_estimate=cost(28),
        name="ffn",
    )(ctx_t, hidden, wo, w12, w12, vec, b1)

def ffn_back_kernel(grad, second, first, slope, w1, w2, wo, gains, douter, dinner, dfirst, dattend, dc, dc_t, sums, b1_sum):
    @pl.when(pl.program_id(0) == 0)
    def _():
        sums[...] = jnp.zeros_like(sums)
        b1_sum[...] = jnp.zeros_like(b1_sum)
    def back(g, x, gain):
        hat, r = centred_rows(x)
        e = g * gain
        return (e - jnp.mean(e, -1, keepdims=True) - hat * jnp.mean(e * hat, -1, keepdims=True)) * r, hat
    def column(v):
        return jnp.sum(v, 0, keepdims=True)
    g = grad[...].astype(F32)
    dsecond, hat = back(g, second[...], gains[4:5, :])
    sums[0:1, :] += column(g * hat)
    sums[1:2, :] += column(g)
    low = dsecond.astype(BF16)
    douter[...] = low
    sums[2:3, :] += column(low.astype(F32))
    dnormed = dsecond
    for j in range(FF // D):
        cols = slice(j * D, (j + 1) * D)
        d = (dot_cols(low, w2[:, cols]) * slope[:, cols].astype(F32)).astype(BF16)
        dinner[:, cols] = d
        b1_sum[:, cols] += column(d.astype(F32))
        dnormed = dnormed + dot_cols(d, w1[:, cols])
    dx, hat = back(dnormed, first[...], gains[1:2, :])
    sums[3:4, :] += column(dnormed * hat)
    sums[4:5, :] += column(dnormed)
    dfirst[...] = dx
    low = dx.astype(BF16)
    dattend[...] = low
    sums[5:6, :] += column(low.astype(F32))
    dc[...] = dot_cols(low, wo[...]).astype(BF16)
    dc_t[...] = dot_cols(wo[...], low).astype(BF16)

def ffn_back(grad, second, first, slope, w12, wo, wo_at, gains):
    n = grad.shape[0]
    row = lambda w: pl.BlockSpec((ROWS, w), lambda i: (i, 0))
    return pl.pallas_call(
        ffn_back_kernel,
        grid=(n // ROWS,),
        in_specs=[row(D), row(D), row(D), row(FF), once((D, FF)), once((D, FF), 1), once((D, D), wo_at), once((8, D))],
        out_specs=[row(D), row(FF), row(D), row(D), row(D), pl.BlockSpec((D, ROWS), lambda i: (0, i)), pl.BlockSpec((8, D), lambda i: (0, 0)), pl.BlockSpec((1, FF), lambda i: (0, 0))],
        out_shape=[jax.ShapeDtypeStruct((n, D), BF16), jax.ShapeDtypeStruct((n, FF), BF16), jax.ShapeDtypeStruct((n, D), F32),
                   jax.ShapeDtypeStruct((n, D), BF16), jax.ShapeDtypeStruct((n, D), BF16), jax.ShapeDtypeStruct((D, n), BF16),
                   jax.ShapeDtypeStruct((8, D), F32), jax.ShapeDtypeStruct((1, FF), F32)],
        compiler_params=pltpu.CompilerParams(vmem_limit_bytes=56 * 2**20),
        cost_estimate=cost(1),
        name="ffn_back",
    )(grad, second, first, slope, w12, w12, wo, gains)

def ffn_grads_kernel(extra, normed, dinner, active, douter, ctx_t, dattend, sums, b1_sum, *rest):
    (other, other_vec, out, turned) = rest if extra else (None, None) + rest
    n = pl.program_id(0)
    blocks = FF // D
    last = 2 * blocks + 1 + extra

    @pl.when(n == 0)
    def _():
        turned[...] = normed[...].T

    @pl.when(n < blocks)
    def _():
        out[...] = dot(turned[...], dinner[...]).astype(BF16)

    @pl.when(jnp.logical_and(n >= blocks, n < 2 * blocks))
    def _():
        out[...] = dot_rows(active[...], douter[...]).astype(BF16)

    @pl.when(n == 2 * blocks)
    def _():
        out[...] = dot(ctx_t[...].astype(BF16), dattend[...]).astype(BF16)

    @pl.when(n == last)
    def _():
        rows = [sums[...]] + [b1_sum[:, j * D : (j + 1) * D] for j in range(blocks)]
        rows = jnp.concatenate(rows + [jnp.zeros((BLK - 8 - blocks, D), F32)], 0)
        out[:, :BLK] = rows.T.astype(BF16)
        if extra:
            out[:, BLK : 2 * BLK] = other_vec[...]

    if extra:

        @pl.when(jnp.logical_and(n > 2 * blocks, n < last))
        def _():
            out[...] = other[...]


def ffn_grads(normed, dinner, active, douter, ctx_t, dattend, sums, b1_sum, other=None):
    n = normed.shape[0]
    blocks = FF // D
    extra = 0 if other is None else 3
    width = (2 * blocks + 1 + extra) * D + (2 if extra else 1) * BLK
    part = lambda first, count: (lambda i: (0, jnp.clip(i - first, 0, count - 1)))
    specs = [
        once((n, D)),
        pl.BlockSpec((n, D), part(0, blocks)),
        pl.BlockSpec((n, D), part(blocks, blocks)),
        once((n, D)),
        once((D, n)),
        once((n, D)),
        once((8, D)),
        once((1, FF)),
    ]
    args = [normed, dinner, active, douter, ctx_t, dattend, sums, b1_sum]
    if extra:
        specs += [pl.BlockSpec((D, D), part(2 * blocks + 1, extra)), once((D, BLK), extra * D // BLK)]
        args += [other, other]
    return pl.pallas_call(
        functools.partial(ffn_grads_kernel, extra),
        grid=(2 * blocks + 2 + extra,),
        in_specs=specs,
        out_specs=pl.BlockSpec((D, D), lambda i: (0, i)),
        out_shape=jax.ShapeDtypeStruct((D, width), BF16),
        scratch_shapes=[pltpu.VMEM((D, n), BF16)],
        compiler_params=pltpu.CompilerParams(vmem_limit_bytes=56 * 2**20),
        cost_estimate=cost(1),
        name="ffn_grads",
    )(*args)


def project_kernel(low, w, qb, vb, q, q_t, k, k_t, v, v_t):
    i = pl.program_id(0)
    n = pl.num_programs(0)
    x = low[...]
    kk = dot(x, w[:, D : 2 * D]).astype(BF16)
    k[...] = kk
    k_t[...] = kk.T
    vv = (dot(x, w[:, 2 * D : 3 * D]) + vb[...]).astype(BF16)
    v[...] = vv
    v_t[...] = vv.T
    skip = RIM * BLK // ROWS

    @pl.when(jnp.logical_and(i >= skip, i < n - skip))
    def _():
        qq = (dot(x, w[:, :D]) + qb[...]).astype(BF16)
        q[...] = qq
        q_t[...] = qq.T

def project(low_ext, w, qb, vb):
    n = low_ext.shape[0]
    rim = RIM * BLK
    skip = rim // ROWS
    own = n - 2 * rim
    last = own // ROWS - 1
    row = pl.BlockSpec((ROWS, D), lambda i: (i, 0))
    col = pl.BlockSpec((D, ROWS), lambda i: (0, i))
    qrow = pl.BlockSpec((ROWS, D), lambda i: (jnp.clip(i - skip, 0, last), 0))
    qcol = pl.BlockSpec((D, ROWS), lambda i: (0, jnp.clip(i - skip, 0, last)))
    tall = jax.ShapeDtypeStruct((n, D), BF16)
    wide = jax.ShapeDtypeStruct((D, n), BF16)
    return pl.pallas_call(
        project_kernel,
        grid=(n // ROWS,),
        in_specs=[row, once((D, 3 * D)), once((1, D)), once((1, D))],
        out_specs=[qrow, qcol, row, col, row, col],
        out_shape=[jax.ShapeDtypeStruct((own, D), BF16), jax.ShapeDtypeStruct((D, own), BF16), tall, wide, tall, wide],
        compiler_params=pltpu.CompilerParams(vmem_limit_bytes=40 * 2**20),
        cost_estimate=cost(14),
        name="project",
    )(low_ext, w, qb, vb)

def att_grads_kernel(low, dq_t, dk, dv, dr, rate, out, turned):
    n = pl.program_id(0)
    own = dq_t.shape[1]
    rim = (low.shape[0] - own) // 2

    @pl.when(n == 0)
    def _():
        turned[...] = low[...].T
        out[...] = dot_cols(turned[:, rim : rim + own], dq_t[...]).astype(BF16)

    @pl.when(n == 1)
    def _():
        out[...] = dot(turned[...], dk[...]).astype(BF16)

    @pl.when(n == 2)
    def _():
        out[...] = dot(turned[...], dv[...]).astype(BF16)

    @pl.when(n == 3)
    def _():
        qb = jnp.sum(dq_t[...].astype(F32), 1, keepdims=True)
        vb = jnp.sum(dv[...].astype(F32), 0, keepdims=True)
        left = lax.broadcasted_iota(jnp.int32, (SPAN * SPAN, BLK), 1) < HD
        columns = []
        for hp in range(PAIRS):
            both = dr[:, hp, :]
            columns.append(jnp.sum(jnp.where(left, both, 0.0), 1, keepdims=True))
            columns.append(jnp.sum(jnp.where(left, 0.0, both), 1, keepdims=True))
        logit = jnp.concatenate(columns, 0) * rate[...]
        rows = jnp.concatenate([vb, jnp.zeros((127, D), F32)], 0).T
        lane = lax.broadcasted_iota(jnp.int32, (D, 128), 1)
        out[:, :128] = jnp.where(lane == 2, qb, jnp.where(lane == 1, logit, rows)).astype(BF16)

def att_grads(low_ext, dq_t, dk, dv, dr, rate):
    n = low_ext.shape[0]
    own = dq_t.shape[1]
    return pl.pallas_call(
        att_grads_kernel,
        grid=(4,),
        in_specs=[once((n, D)), once((D, own)), once((n, D)), once((n, D)), once(dr.shape), once((D, 1))],
        out_specs=pl.BlockSpec((D, D), lambda i: (0, i)),
        out_shape=jax.ShapeDtypeStruct((D, 3 * D + 128), BF16),
        scratch_shapes=[pltpu.VMEM((D, n), BF16)],
        compiler_params=pltpu.CompilerParams(vmem_limit_bytes=48 * 2**20),
        cost_estimate=cost(1),
        name="att_grads",
    )(low_ext, dq_t, dk, dv, dr, rate)

def input_back_kernel(dk, dv, dq_t, dfirst, w, own, rims):
    i = pl.program_id(0)
    n = pl.num_programs(0)
    skip = RIM * BLK // ROWS
    total = dot_cols(dk[...], w[:, D : 2 * D]) + dot_cols(dv[...], w[:, 2 * D : 3 * D])
    inside = jnp.logical_and(i >= skip, i < n - skip)

    @pl.when(inside)
    def _():
        own[...] = total + dot_tt(dq_t[...], w[:, :D]) + dfirst[...]

    @pl.when(jnp.logical_not(inside))
    def _():
        rims[...] = total.astype(BF16)

def input_back(dk, dv, dq_t, dfirst, w):
    n = dk.shape[0]
    own = dfirst.shape[0]
    skip = (n - own) // 2 // ROWS
    last = own // ROWS - 1
    row = pl.BlockSpec((ROWS, D), lambda i: (i, 0))
    orow = pl.BlockSpec((ROWS, D), lambda i: (jnp.clip(i - skip, 0, last), 0))
    ocol = pl.BlockSpec((D, ROWS), lambda i: (0, jnp.clip(i - skip, 0, last)))
    rrow = pl.BlockSpec((ROWS, D), lambda i: (jnp.where(i < skip, i, jnp.maximum(i - last - 1, skip)), 0))
    return pl.pallas_call(
        input_back_kernel,
        grid=(n // ROWS,),
        in_specs=[row, row, ocol, orow, once((D, 3 * D))],
        out_specs=[orow, rrow],
        out_shape=[jax.ShapeDtypeStruct((own, D), F32), jax.ShapeDtypeStruct((n - own, D), BF16)],
        compiler_params=pltpu.CompilerParams(vmem_limit_bytes=40 * 2**20),
        cost_estimate=cost(1),
        name="input_back",
    )(dk, dv, dq_t, dfirst, w)


def neighbours(tail, head):
    count = lax.axis_size("dp")
    return (
        lax.ppermute(tail, "dp", [(i, i + 1) for i in range(count - 1)]),
        lax.ppermute(head, "dp", [(i + 1, i) for i in range(count - 1)]),
    )


def gathered(part):
    return lax.all_gather(part, AXES, axis=0, tiled=True)


def place():
    dp = lax.axis_index("dp")
    mp = lax.axis_index("mp")
    return dp // 2, (dp % 2) * (lax.axis_size("mp") // 2) + mp // 2, mp % 2


def sizes():
    return lax.axis_size("dp") // 2, lax.axis_size("mp")


def swap(block, mask):
    count = lax.axis_size("dp") * lax.axis_size("mp")
    return lax.ppermute(block, AXES, [(i, i ^ mask) for i in range(count)])


def put(buffer, piece, index):
    return lax.dynamic_update_slice(buffer, piece[None], (index,) + (0,) * piece.ndim)


class SteppedGather:
    def __init__(self, part):
        self.part = part
        self.block = part
        self.step = 0

    def settle(self, tied):
        if self.step > 0:
            own = place()[self.step - 1]
            out = jnp.zeros((len(self.arriving) + 1,) + self.block.shape, self.block.dtype)
            tied, out = lax.optimization_barrier((tied, out))
            out = put(out, self.block, own)
            for d, piece in self.arriving:
                out = put(out, piece, own ^ d)
            self.block = out
        return tied

    def advance(self, tied):
        far, middle = sizes()
        tied = self.settle(tied)
        tied, self.block = lax.optimization_barrier((tied, self.block))
        self.step += 1
        count, scale = ((far, 2 * middle), (middle, 2), (2, 1))[self.step - 1]
        self.arriving = [(d, swap(self.block, d * scale)) for d in range(1, count)]
        return tied

    def result(self, tied):
        self.settle(tied)
        return self.block.transpose(2, 1, 0, 3, 4).reshape(-1, self.part.shape[1])


def scattered(part):
    return lax.psum_scatter(part, AXES, scatter_dimension=0, tiled=True).astype(F32)


def pick(array, index, axis):
    return lax.dynamic_index_in_dim(array, index, axis, keepdims=False)


class SteppedSum:
    def __init__(self, part):
        far, middle = sizes()
        self.parts = part.reshape(far, middle, 2, -1, part.shape[1])
        self.step = 0

    def anchored(self, tied):
        tied, kept = lax.optimization_barrier((tied, self.halves[0]))
        return tied, (kept, self.halves[1])

    def middle_sum(self, index):
        kept, got = self.halves
        return pick(kept, index, 1).astype(F32) + pick(got, index, 1).astype(F32)

    def far_sum(self, index):
        z, m, c = place()
        total = self.middle_own(index)
        for piece in self.arrived:
            total = total + pick(piece, index, 0).astype(F32)
        return total

    def middle_own(self, index):
        z, m, c = place()
        kept, got = self.halves
        return pick(pick(kept, m, 1), index, 0).astype(F32) + pick(
            pick(got, m, 1), index, 0
        ).astype(F32)

    def advance(self, tied):
        far, middle = sizes()
        z, m, c = place()
        self.step += 1
        if self.step == 1:
            out = pick(self.parts, 1 - c, 2)
            tied, out = lax.optimization_barrier((tied, out))
            self.halves = (pick(self.parts, c, 2), swap(out, 1))
        elif self.step == 2:
            tied, self.halves = self.anchored(tied)
            out = [self.middle_sum(m ^ d).astype(BF16) for d in range(1, middle)]
            tied, out = lax.optimization_barrier((tied, out))
            self.arrived = [swap(item, d * 2) for d, item in zip(range(1, middle), out)]
        else:
            tied, self.halves = self.anchored(tied)
            out = [self.far_sum(z ^ d).astype(BF16) for d in range(1, far)]
            tied, out = lax.optimization_barrier((tied, out))
            self.last = [swap(item, d * 2 * middle) for d, item in zip(range(1, far), out)]
        return tied

    def result(self):
        z, m, c = place()
        total = self.far_sum(z)
        for piece in self.last:
            total = total + piece.astype(F32)
        return total


def table_rows(table):
    rows = table.reshape(PAIRS, 2, SPAN * SPAN).transpose(2, 0, 1)
    return jnp.repeat(rows, BLK, axis=2)


def layer_forward(hidden, low_ext, head, vec, flags, keep, temper, pos, before, between):
    z = (vec["logits"] + vec["jitter"]).reshape(HEADS, SPAN, SPAN) / temper[:, None, None]
    relaxed = jax.nn.sigmoid(z)
    factor = table_rows(relaxed)
    q, q_t, k, k_t, v, v_t = project(low_ext, head, vec["qb"][None], vec["vb"][None])
    q_t = before(q_t)
    log_factor, inv_factor = jnp.log2(factor), 1.0 / factor
    ctx_t, lse = attend(flags, keep, pos, factor, q_t, k, v_t)
    ctx_t, wo, wo_at, w12 = between(ctx_t)
    names = ("ob", "g1", "s1", "b2", "g2", "s2", "s2", "s2")
    vectors = jnp.stack([vec[name] for name in names])
    first, normed_low, active, slope, second, result, result_low = ffn(
        ctx_t, hidden, wo, wo_at, w12, vectors, vec["b1"][None]
    )
    record = (low_ext, q, q_t, k, k_t, v, ctx_t, lse, first, normed_low, active, slope, second)
    return result, result_low, record + (relaxed, log_factor, inv_factor, vectors, head, wo, wo_at, w12)


def layer_backward(grad, record, flags, keep, temper, pos, before=None, done=None):
    low_ext, q, q_t, k, k_t, v, ctx_t, lse, first, normed_low, active, slope, second = record[:13]
    relaxed, log_factor, inv_factor, vectors, head, wo, wo_at, w12 = record[13:]
    rows = first.shape[0]
    rim = RIM * BLK
    douter, dinner, dfirst, dattend, dc, dc_t, row_sums, b1_sum = ffn_back(
        grad, second, first, slope, w12, wo, wo_at, vectors
    )
    part = ffn_grads(normed_low, dinner, active, douter, ctx_t, dattend, row_sums, b1_sum, before)
    if before is None:
        dc, part = lax.optimization_barrier((dc, part))
        ffn_sum = scattered(part)
    else:
        ffn_sum = SteppedSum(part)
        dc = ffn_sum.advance(dc)
        dc = ffn_sum.advance(dc)
    dq_t, dk, dv, dr = attend_back(
        flags, keep, pos, log_factor, inv_factor, q_t, q, dc_t, dc, ctx_t, lse, k, k_t, v
    )
    rate = ((1.0 - relaxed) / temper[:, None, None]).reshape(-1, 1)
    if before is None:
        own, rims = input_back(dk, dv, dq_t, dfirst, head)
        from_lower, from_upper = neighbours(rims[rim:], rims[:rim])
        dq_t, rims = lax.optimization_barrier((dq_t, rims))
        att_sum = att_grads(low_ext, dq_t, dk, dv, dr, rate)
    else:
        att_sum = SteppedSum(att_grads(low_ext, dq_t, dk, dv, dr, rate))
        dk = att_sum.advance(dk)
        dk, done = lax.optimization_barrier((dk, done))
        dk = ffn_sum.advance(dk)
        own, rims = input_back(dk, dv, dq_t, dfirst, head)
        own = att_sum.advance(own)
        from_lower, from_upper = neighbours(rims[rim:], rims[:rim])
        own = att_sum.advance(own)
    dhidden = own.at[:rim].add(from_lower.astype(F32))
    dhidden = dhidden.at[rows - rim :].add(from_upper.astype(F32))
    return dhidden, ffn_sum, att_sum, done


def per_device(
    embedded,
    opening,
    selector,
    wq,
    wk,
    wv,
    wo,
    qb,
    vb,
    ob,
    g1,
    s1,
    w1,
    b1,
    w2,
    b2,
    g2,
    s2,
    scores,
    jitter,
    warmth,
    upstream,
):
    share = wq.shape[1]
    devices = D // share
    flags = opening[0]
    pos = lax.axis_index("dp").reshape(1).astype(jnp.int32)
    rim = RIM * BLK

    def widened(part):
        lead = part.shape[:-1]
        return jnp.swapaxes(part.reshape(lead + (devices, 4, share)), -3, -2).reshape(lead + (FF,))

    def own_parts(tier):
        narrow = w2[tier].reshape(4, share, D)
        vectors = jnp.stack(
            [item[tier] for item in (qb, vb, ob, g1, s1, b2, g2, s2, scores, jitter)]
            + [b1[tier].reshape(4, share)[j] for j in range(4)],
            1,
        )
        vectors = jnp.pad(vectors, ((0, 0), (0, 128 - vectors.shape[1])))
        first = [wq[tier], wk[tier], wv[tier]]
        wide = [widened(w1[tier])] + [narrow[j] for j in range(4)]
        return first, wide, [wo[tier]], [vectors]

    def unpacked(columns):
        columns = jnp.transpose(columns.astype(F32))
        names = ("qb", "vb", "ob", "g1", "s1", "b2", "g2", "s2", "logits", "jitter")
        vec = {name: columns[n] for n, name in enumerate(names)}
        vec["b1"] = columns[len(names) : len(names) + 4].reshape(FF)
        return vec

    symbols = embedded[0]
    first, wide, out, vectors = own_parts(0)
    gather = SteppedGather(jnp.concatenate(first + vectors, 1))
    symbols = gather.advance(symbols)
    symbols, rest = lax.optimization_barrier((symbols, jnp.concatenate(wide + out, 1)))
    symbols = gather.advance(gather.advance(symbols))
    lower, upper = neighbours(symbols[symbols.shape[0] - rim :], symbols[:rim])
    low_ext = jnp.concatenate([lower, symbols, upper], 0)
    head_zero = gather.result(symbols)
    head_zero, rest = lax.optimization_barrier((head_zero, rest))
    tail_zero = gathered(rest)
    first, wide, out, vectors = own_parts(1)
    later = SteppedGather(jnp.concatenate(first + out + vectors, 1))
    tails = []

    def between_zero(ctx_t):
        ctx_t = later.advance(ctx_t)
        _, _, *rest = lax.optimization_barrier((ctx_t, tail_zero, *wide))
        tails.append(gathered(jnp.concatenate(rest, 1)))
        return ctx_t, tail_zero, 2 * FF // D, tail_zero

    def between_one(ctx_t):
        return ctx_t, head_one, 3, tails[0]

    hidden, low, record = layer_forward(
        symbols,
        low_ext,
        head_zero,
        unpacked(head_zero[:, 3 * D :]),
        flags,
        selector[0, 0],
        warmth[0],
        pos,
        later.advance,
        between_zero,
    )
    records = [record]
    low = later.advance(low)
    lower, upper = neighbours(low[low.shape[0] - rim :], low[:rim])
    low_ext = jnp.concatenate([lower, low, upper], 0)
    head_one = later.result(low)
    hidden, _, record = layer_forward(
        hidden,
        low_ext,
        head_one,
        unpacked(head_one[:, 4 * D :]),
        flags,
        selector[1, 0],
        warmth[1],
        pos,
        lambda q_t: q_t,
        between_one,
    )
    records.append(record)
    grad = upstream[0]
    grad, ffn_one, att_one, _ = layer_backward(
        grad, records[1], flags, selector[1, 0], warmth[1], pos
    )
    grad, ffn_zero, att_zero, ffn_one = layer_backward(
        grad, records[0], flags, selector[0, 0], warmth[0], pos, att_one, ffn_one
    )
    both = ffn_zero.result()
    last = att_zero.result()
    ends = [2 * FF + D, 2 * FF + 4 * D]
    fv = jnp.stack([both[:, ends[1] : ends[1] + BLK], ffn_one[:, ends[0] :]])
    av = jnp.stack([last[:, 3 * D :], both[:, ends[1] + BLK :]])
    ffn_sums = jnp.stack([both[:, : ends[0]], ffn_one[:, : ends[0]]])
    att = jnp.stack([last[:, : 3 * D], both[:, ends[0] : ends[1]]])
    w1_grad = unwiden(both, ffn_one)
    w2_grad = jnp.concatenate([ffn_sums[:, :, FF + j * D : FF + (j + 1) * D] for j in range(4)], 1)
    wo_grad = ffn_sums[:, :, 2 * FF :]
    b1_grad = jnp.concatenate([fv[:, :, 8 + j] for j in range(4)], 1)
    new_mask = (scores.astype(F32) + jitter.astype(F32) > 0).astype(jnp.int32)
    return (
        hidden[None],
        grad[None],
        att[:, :, :D],
        att[:, :, D : 2 * D],
        att[:, :, 2 * D : 3 * D],
        wo_grad,
        av[:, :, 2],
        av[:, :, 0],
        fv[:, :, 5],
        fv[:, :, 3],
        fv[:, :, 4],
        w1_grad,
        b1_grad,
        w2_grad,
        fv[:, :, 2],
        fv[:, :, 0],
        fv[:, :, 1],
        av[:, :, 1],
        new_mask,
    )


def solution(mesh):
    rows = P("mp", "dp", None)
    matrix = P(None, AXES, None)
    vector = P(None, AXES)
    return jax.shard_map(
        per_device,
        mesh=mesh,
        in_specs=(rows, P("mp", None), P(None, "mp", "dp", None))
        + (matrix,) * 4
        + (vector,) * 5
        + (matrix, vector, matrix)
        + (vector,) * 5
        + (P(), rows),
        out_specs=(rows, rows)
        + (matrix,) * 4
        + (vector,) * 5
        + (matrix, vector, matrix)
        + (vector,) * 5,
        check_vma=False,
    )
```

```python
import functools
import math

import jax
import jax.numpy as jnp
from jax import lax
from jax.experimental import pallas as pl
from jax.experimental.pallas import tpu as pltpu
from jax.sharding import PartitionSpec as P

D = 768
HEADS = 12
HD = 64
FF = 3072
BLK = 128
SPAN = 8
RIM = 4
PAIRS = HEADS // 2
AXES = ("dp", "mp")
SCALE = HD**-0.5
SCALE2 = SCALE * math.log2(math.e)
F32 = jnp.float32
BF16 = jnp.bfloat16


def cost(us):
    return pl.CostEstimate(flops=int(us * 1e9), bytes_accessed=1_000_000, transcendentals=0)


def once(shape, column=0):
    return pl.BlockSpec(shape, lambda i: (0,) * (len(shape) - 1) + (column,), pipeline_mode=pl.Buffered(1))


def dot(a, b):
    return jnp.dot(a, b, preferred_element_type=F32)


def dot_rows(a, b):
    return lax.dot_general(a, b, (((0,), (0,)), ((), ())), preferred_element_type=F32)


def dot_cols(a, b):
    return lax.dot_general(a, b, (((1,), (1,)), ((), ())), preferred_element_type=F32)


def dot_tt(a, b):
    return lax.dot_general(a, b, (((0,), (1,)), ((), ())), preferred_element_type=F32)


def scan_blocks(flags, pos, first_s, last_s, own):
    ext = own + 2 * RIM
    total = flags.shape[0]
    base = pos * own - RIM

    def opens(e):
        gid = base + e
        inside = jnp.logical_and(gid >= 0, gid < total)
        return jnp.where(inside, flags[jnp.clip(gid, 0, total - 1)], 1)

    def up(e, start):
        start = jnp.where(opens(e) == 1, e, start)
        first_s[e] = start
        return start

    lax.fori_loop(0, ext, up, jnp.int32(0))

    def down(n, stop):
        e = ext - 1 - n
        last_s[e] = stop
        return jnp.where(opens(e) == 1, e, stop)

    lax.fori_loop(0, ext, down, jnp.int32(ext))


def list_kept(keep, i, first_s, last_s, kept_s):
    me = i + RIM

    def one(e, count):
        wanted = jnp.logical_or(e == me, keep[i, jnp.clip(e - me + SPAN - 1, 0, 2 * SPAN - 2)] > 0)

        @pl.when(wanted)
        def _():
            kept_s[count] = e

        return count + wanted.astype(jnp.int32)

    return lax.fori_loop(first_s[me], last_s[me], one, jnp.int32(0))


def two_kept(n, count, kept_s, start, me):
    out = []
    for e in (kept_s[2 * n], kept_s[jnp.minimum(2 * n + 1, count - 1)]):
        rows = pl.ds(pl.multiple_of(e * BLK, BLK), BLK)
        out.append((rows, (me - start) * SPAN + (e - start)))
    void = jnp.where(2 * n + 1 < count, 0.0, -1e30).astype(F32)
    return out, void


def forward_kernel(
    flags, keep, pos, factor, q_t, k, v_t, ctx_t, lse, qbd, acc, top, total, first_s, last_s
):
    own = q_t.shape[1] // BLK
    scan_blocks(flags, pos[0], first_s, last_s, own)
    qbd[...] = jnp.zeros_like(qbd)

    @pl.loop(0, own)
    def _(i):
        cols = pl.ds(pl.multiple_of(i * BLK, BLK), BLK)
        for hp in range(PAIRS):
            qbd[hp, :HD, :BLK] = q_t[pl.ds(hp * BLK, HD), cols]
            qbd[hp, HD:, BLK:] = q_t[pl.ds(hp * BLK + HD, HD), cols]
        acc[...] = jnp.zeros_like(acc)
        top[...] = jnp.full_like(top, -1e30)
        total[...] = jnp.zeros_like(total)
        me = i + RIM
        start = first_s[me]

        @pl.loop(start, last_s[me])
        def _(e):
            wanted = jnp.logical_or(e == me, keep[i, jnp.clip(e - me + SPAN - 1, 0, 2 * SPAN - 2)] > 0)

            @pl.when(wanted)
            def _():
                rows = pl.ds(pl.multiple_of(e * BLK, BLK), BLK)
                ab = (me - start) * SPAN + (e - start)
                for hp in range(PAIRS):
                    lanes = slice(hp * BLK, (hp + 1) * BLK)
                    s = dot(k[rows, lanes], qbd[hp])
                    m_old = top[hp : hp + 1, :]
                    m_new = jnp.maximum(m_old, jnp.max(s, axis=0, keepdims=True))
                    p = jnp.exp2((s - m_new) * SCALE2)
                    alpha = jnp.exp2((m_old - m_new) * SCALE2)
                    total[hp : hp + 1, :] = total[hp : hp + 1, :] * alpha + jnp.sum(
                        p, axis=0, keepdims=True
                    )
                    top[hp : hp + 1, :] = m_new
                    c = dot(v_t[lanes, rows], p.astype(BF16))
                    f = factor[ab, hp : hp + 1, :]
                    upper = slice(hp * BLK, hp * BLK + HD)
                    lower = slice(hp * BLK + HD, (hp + 1) * BLK)
                    acc[upper, :] = acc[upper, :] * alpha[:, :BLK] + c[:HD, :BLK] * f[:, :BLK]
                    acc[lower, :] = acc[lower, :] * alpha[:, BLK:] + c[HD:, BLK:] * f[:, BLK:]

        for hp in range(PAIRS):
            t = total[hp : hp + 1, :]
            r = 1.0 / t
            upper = slice(hp * BLK, hp * BLK + HD)
            lower = slice(hp * BLK + HD, (hp + 1) * BLK)
            ctx_t[upper, cols] = acc[upper, :] * r[:, :BLK]
            ctx_t[lower, cols] = acc[lower, :] * r[:, BLK:]
            lse[i, hp : hp + 1, :] = top[hp : hp + 1, :] * SCALE2 + jnp.log2(t)


def smem():
    return pl.BlockSpec(memory_space=pltpu.SMEM)


def vmem():
    return pl.BlockSpec(memory_space=pltpu.VMEM)


def unwiden_kernel(a, b, out):
    share = a.shape[0]
    for n, ref in enumerate((a, b)):
        for d in range(D // share):
            pieces = [ref[:, j * D + share * d : j * D + share * (d + 1)] for j in range(FF // D)]
            for j, piece in enumerate(pieces):
                at = FF // D * share * d + share * j
                out[n, :, at : at + share] = piece


def unwiden(a, b):
    share = a.shape[0]
    return pl.pallas_call(
        unwiden_kernel,
        grid=(1,),
        in_specs=[pl.BlockSpec((share, FF), lambda i: (0, 0))] * 2,
        out_specs=pl.BlockSpec((2, share, FF), lambda i: (0, 0, 0)),
        out_shape=jax.ShapeDtypeStruct((2, share, FF), F32),
        cost_estimate=cost(2),
        name="unwiden",
    )(a, b)


def attend(flags, keep, pos, factor, q_t, k, v_t):
    own = q_t.shape[1] // BLK
    ext = own + 2 * RIM
    return pl.pallas_call(
        forward_kernel,
        out_shape=(
            jax.ShapeDtypeStruct(q_t.shape, F32),
            jax.ShapeDtypeStruct((own, 8, 2 * BLK), F32),
        ),
        in_specs=[smem(), smem(), smem(), vmem(), vmem(), vmem(), vmem()],
        out_specs=(vmem(), vmem()),
        scratch_shapes=[
            pltpu.VMEM((PAIRS, BLK, 2 * BLK), BF16),
            pltpu.VMEM((D, BLK), F32),
            pltpu.VMEM((8, 2 * BLK), F32),
            pltpu.VMEM((8, 2 * BLK), F32),
            pltpu.SMEM((ext,), jnp.int32),
            pltpu.SMEM((ext,), jnp.int32),
        ],
        compiler_params=pltpu.CompilerParams(vmem_limit_bytes=40 * 2**20),
        cost_estimate=cost(13),
        name="attend",
    )(flags, keep, pos, factor, q_t, k, v_t)


def backward_kernel(
    flags,
    keep,
    pos,
    log_factor,
    inv_factor,
    q_t,
    q,
    dc_t,
    dc,
    ctx_t,
    lse,
    k,
    k_t,
    v,
    dq_t,
    dk,
    dv,
    dr,
    qbd,
    cbd,
    q2,
    c2,
    dq_acc,
    dk_acc,
    dv_acc,
    delta,
    first_s,
    last_s,
    kept_s,
):
    own = q_t.shape[1] // BLK
    scan_blocks(flags, pos[0], first_s, last_s, own)
    qbd[...] = jnp.zeros_like(qbd)
    cbd[...] = jnp.zeros_like(cbd)
    dk_acc[...] = jnp.zeros_like(dk_acc)
    dv_acc[...] = jnp.zeros_like(dv_acc)
    dr[...] = jnp.zeros_like(dr)
    left = lax.broadcasted_iota(jnp.int32, (BLK, BLK), 1) < HD

    @pl.loop(0, own)
    def _(i):
        cols = pl.ds(pl.multiple_of(i * BLK, BLK), BLK)
        for hp in range(PAIRS):
            lanes = slice(hp * BLK, (hp + 1) * BLK)
            upper = pl.ds(hp * BLK, HD)
            lower = pl.ds(hp * BLK + HD, HD)
            qbd[hp, :HD, :BLK] = q_t[upper, cols]
            qbd[hp, HD:, BLK:] = q_t[lower, cols]
            cu = dc_t[upper, cols]
            cl = dc_t[lower, cols]
            cbd[hp, :HD, :BLK] = cu
            cbd[hp, HD:, BLK:] = cl
            delta[hp : hp + 1, :BLK] = jnp.sum(
                cu.astype(F32) * ctx_t[upper, cols], axis=0, keepdims=True
            )
            delta[hp : hp + 1, BLK:] = jnp.sum(
                cl.astype(F32) * ctx_t[lower, cols], axis=0, keepdims=True
            )
            qn = q[cols, lanes].astype(F32)
            cn = dc[cols, lanes].astype(F32)
            q2[hp, :BLK, :] = jnp.where(left, qn, 0.0).astype(BF16)
            q2[hp, BLK:, :] = jnp.where(left, 0.0, qn).astype(BF16)
            c2[hp, :BLK, :] = jnp.where(left, cn, 0.0).astype(BF16)
            c2[hp, BLK:, :] = jnp.where(left, 0.0, cn).astype(BF16)
        dq_acc[...] = jnp.zeros_like(dq_acc)
        me = i + RIM
        count = list_kept(keep, i, first_s, last_s, kept_s)

        @pl.loop(0, (count + 1) // 2)
        def _(n):
            ((rows_a, ab_a), (rows_b, ab_b)), void = two_kept(n, count, kept_s, first_s[me], me)
            for hp in range(PAIRS):
                lanes = slice(hp * BLK, (hp + 1) * BLK)
                one = slice(hp, hp + 1)
                vb = jnp.concatenate([v[rows_a, lanes], v[rows_b, lanes]], 0)
                s = dot(jnp.concatenate([k[rows_a, lanes], k[rows_b, lanes]], 0), qbd[hp])
                dw = dot(vb, cbd[hp])
                level = lse[i, one, :]
                w_a = jnp.exp2(s[:BLK] * SCALE2 + (log_factor[ab_a, one, :] - level))
                w_b = jnp.exp2(s[BLK:] * SCALE2 + (log_factor[ab_b, one, :] - level + void))
                ds_a = w_a * (dw[:BLK] - delta[one, :] * inv_factor[ab_a, one, :])
                ds_b = w_b * (dw[BLK:] - delta[one, :] * inv_factor[ab_b, one, :])
                wb = jnp.concatenate([w_a.astype(BF16), w_b.astype(BF16)], 0)
                dsb = jnp.concatenate([ds_a.astype(BF16), ds_b.astype(BF16)], 0)
                dvc = dot(wb, c2[hp])
                dkc = dot(dsb, q2[hp])
                dqc = dot(jnp.concatenate([k_t[lanes, rows_a], k_t[lanes, rows_b]], 1), dsb)
                dv_acc[rows_a, lanes] += dvc[:BLK]
                dv_acc[rows_b, lanes] += dvc[BLK:]
                dk_acc[rows_a, lanes] += dkc[:BLK]
                dk_acc[rows_b, lanes] += dkc[BLK:]
                upper = slice(hp * BLK, hp * BLK + HD)
                lower = slice(hp * BLK + HD, (hp + 1) * BLK)
                dq_acc[upper, :] += dqc[:HD, :BLK]
                dq_acc[lower, :] += dqc[HD:, BLK:]
                dots = dvc * vb.astype(F32)
                dr[ab_a, one, :] += jnp.sum(dots[:BLK], axis=0, keepdims=True)
                dr[ab_b, one, :] += jnp.sum(dots[BLK:], axis=0, keepdims=True)

        dq_t[:, cols] = (dq_acc[...] * SCALE).astype(BF16)

    ext = dk.shape[0] // BLK

    @pl.loop(0, ext)
    def _(e):
        rows = pl.ds(pl.multiple_of(e * BLK, BLK), BLK)
        dk[rows, :] = (dk_acc[rows, :] * SCALE).astype(BF16)
        dv[rows, :] = dv_acc[rows, :].astype(BF16)


def attend_back(flags, keep, pos, log_factor, inv_factor, q_t, q, dc_t, dc, ctx_t, lse, k, k_t, v):
    own = q_t.shape[1] // BLK
    ext = own + 2 * RIM
    return pl.pallas_call(
        backward_kernel,
        out_shape=(
            jax.ShapeDtypeStruct(q_t.shape, BF16),
            jax.ShapeDtypeStruct(k.shape, BF16),
            jax.ShapeDtypeStruct(v.shape, BF16),
            jax.ShapeDtypeStruct((SPAN * SPAN, 8, BLK), F32),
        ),
        in_specs=[smem()] * 3 + [vmem()] * 11,
        out_specs=(vmem(),) * 4,
        scratch_shapes=[
            pltpu.VMEM((PAIRS, BLK, 2 * BLK), BF16),
            pltpu.VMEM((PAIRS, BLK, 2 * BLK), BF16),
            pltpu.VMEM((PAIRS, 2 * BLK, BLK), BF16),
            pltpu.VMEM((PAIRS, 2 * BLK, BLK), BF16),
            pltpu.VMEM((D, BLK), F32),
            pltpu.VMEM((ext * BLK, D), F32),
            pltpu.VMEM((ext * BLK, D), F32),
            pltpu.VMEM((8, 2 * BLK), F32),
            pltpu.SMEM((ext,), jnp.int32),
            pltpu.SMEM((ext,), jnp.int32),
            pltpu.SMEM((ext,), jnp.int32),
        ],
        compiler_params=pltpu.CompilerParams(vmem_limit_bytes=56 * 2**20),
        cost_estimate=cost(1),
        name="attend_back",
    )(flags, keep, pos, log_factor, inv_factor, q_t, q, dc_t, dc, ctx_t, lse, k, k_t, v)


def centred_rows(x):
    middle = jnp.mean(x, -1, keepdims=True)
    c = x - middle
    spread = jnp.mean(c * c, -1, keepdims=True)
    r = lax.rsqrt(spread + 1e-06)
    return c * r, r

def gelu_and_slope(v):
    e = jnp.exp2(v * v * (-0.5 * math.log2(math.e)))
    t = 1.0 / (1.0 + jnp.abs(v) * (0.3275911 * math.sqrt(0.5)))
    q = t * (0.127414796 + t * (-0.142248368 + t * (0.7107068705 + t * (-0.7265760135 + t * 0.5307027145)))) * e
    phi = jnp.where(v >= 0, 1.0 - q, q)
    return v * phi, phi + v * (e * (1.0 / math.sqrt(2.0 * math.pi)))

ROWS = 256

def ffn_kernel(ctx_t, hidden, wo, w1, w2, vec, b1, first, normed_low, active, slope, second, result, result_low):
    x = hidden[...].astype(F32) + dot_rows(ctx_t[...].astype(BF16), wo[...]) + vec[0:1, :]
    first[...] = x
    hat, _ = centred_rows(x)
    normed = hat * vec[1:2, :] + vec[2:3, :]
    low = normed.astype(BF16)
    normed_low[...] = low
    total = normed + vec[3:4, :]
    for j in range(FF // D):
        cols = slice(j * D, (j + 1) * D)
        inner = dot(low, w1[:, cols]) + b1[:, cols]
        a, s = gelu_and_slope(inner)
        a = a.astype(BF16)
        active[:, cols] = a
        slope[:, cols] = s.astype(BF16)
        total = total + dot(a, w2[:, cols])
    second[...] = total
    hat, _ = centred_rows(total)
    x = hat * vec[4:5, :] + vec[5:6, :]
    result[...] = x
    result_low[...] = x.astype(BF16)

def ffn(ctx_t, hidden, wo, wo_at, w12, vec, b1):
    n = hidden.shape[0]
    row = lambda w: pl.BlockSpec((ROWS, w), lambda i: (i, 0))
    return pl.pallas_call(
        ffn_kernel,
        grid=(n // ROWS,),
        in_specs=[pl.BlockSpec((D, ROWS), lambda i: (0, i)), row(D), once((D, D), wo_at), once((D, FF)), once((D, FF), 1), once((8, D)), once((1, FF))],
        out_specs=[row(D), row(D), row(FF), row(FF), row(D), row(D), row(D)],
        out_shape=[jax.ShapeDtypeStruct((n, D), F32), jax.ShapeDtypeStruct((n, D), BF16), jax.ShapeDtypeStruct((n, FF), BF16),
                   jax.ShapeDtypeStruct((n, FF), BF16), jax.ShapeDtypeStruct((n, D), F32), jax.ShapeDtypeStruct((n, D), F32), jax.ShapeDtypeStruct((n, D), BF16)],
        compiler_params=pltpu.CompilerParams(vmem_limit_bytes=56 * 2**20),
        cost_estimate=cost(28),
        name="ffn",
    )(ctx_t, hidden, wo, w12, w12, vec, b1)

def ffn_back_kernel(grad, second, first, slope, w1, w2, wo, gains, douter, dinner, dfirst, dattend, dc, dc_t, sums, b1_sum):
    @pl.when(pl.program_id(0) == 0)
    def _():
        sums[...] = jnp.zeros_like(sums)
        b1_sum[...] = jnp.zeros_like(b1_sum)
    def back(g, x, gain):
        hat, r = centred_rows(x)
        e = g * gain
        return (e - jnp.mean(e, -1, keepdims=True) - hat * jnp.mean(e * hat, -1, keepdims=True)) * r, hat
    def column(v):
        return jnp.sum(v, 0, keepdims=True)
    g = grad[...].astype(F32)
    dsecond, hat = back(g, second[...], gains[4:5, :])
    sums[0:1, :] += column(g * hat)
    sums[1:2, :] += column(g)
    low = dsecond.astype(BF16)
    douter[...] = low
    sums[2:3, :] += column(low.astype(F32))
    dnormed = dsecond
    for j in range(FF // D):
        cols = slice(j * D, (j + 1) * D)
        d = (dot_cols(low, w2[:, cols]) * slope[:, cols].astype(F32)).astype(BF16)
        dinner[:, cols] = d
        b1_sum[:, cols] += column(d.astype(F32))
        dnormed = dnormed + dot_cols(d, w1[:, cols])
    dx, hat = back(dnormed, first[...], gains[1:2, :])
    sums[3:4, :] += column(dnormed * hat)
    sums[4:5, :] += column(dnormed)
    dfirst[...] = dx
    low = dx.astype(BF16)
    dattend[...] = low
    sums[5:6, :] += column(low.astype(F32))
    dc[...] = dot_cols(low, wo[...]).astype(BF16)
    dc_t[...] = dot_cols(wo[...], low).astype(BF16)

def ffn_back(grad, second, first, slope, w12, wo, wo_at, gains):
    n = grad.shape[0]
    row = lambda w: pl.BlockSpec((ROWS, w), lambda i: (i, 0))
    return pl.pallas_call(
        ffn_back_kernel,
        grid=(n // ROWS,),
        in_specs=[row(D), row(D), row(D), row(FF), once((D, FF)), once((D, FF), 1), once((D, D), wo_at), once((8, D))],
        out_specs=[row(D), row(FF), row(D), row(D), row(D), pl.BlockSpec((D, ROWS), lambda i: (0, i)), pl.BlockSpec((8, D), lambda i: (0, 0)), pl.BlockSpec((1, FF), lambda i: (0, 0))],
        out_shape=[jax.ShapeDtypeStruct((n, D), BF16), jax.ShapeDtypeStruct((n, FF), BF16), jax.ShapeDtypeStruct((n, D), F32),
                   jax.ShapeDtypeStruct((n, D), BF16), jax.ShapeDtypeStruct((n, D), BF16), jax.ShapeDtypeStruct((D, n), BF16),
                   jax.ShapeDtypeStruct((8, D), F32), jax.ShapeDtypeStruct((1, FF), F32)],
        compiler_params=pltpu.CompilerParams(vmem_limit_bytes=56 * 2**20),
        cost_estimate=cost(1),
        name="ffn_back",
    )(grad, second, first, slope, w12, w12, wo, gains)

def ffn_grads_kernel(extra, normed, dinner, active, douter, ctx_t, dattend, sums, b1_sum, *rest):
    (other, other_vec, out, turned) = rest if extra else (None, None) + rest
    n = pl.program_id(0)
    blocks = FF // D
    last = 2 * blocks + 1 + extra

    @pl.when(n == 0)
    def _():
        turned[...] = normed[...].T

    @pl.when(n < blocks)
    def _():
        out[...] = dot(turned[...], dinner[...]).astype(BF16)

    @pl.when(jnp.logical_and(n >= blocks, n < 2 * blocks))
    def _():
        out[...] = dot_rows(active[...], douter[...]).astype(BF16)

    @pl.when(n == 2 * blocks)
    def _():
        out[...] = dot(ctx_t[...].astype(BF16), dattend[...]).astype(BF16)

    @pl.when(n == last)
    def _():
        rows = [sums[...]] + [b1_sum[:, j * D : (j + 1) * D] for j in range(blocks)]
        rows = jnp.concatenate(rows + [jnp.zeros((BLK - 8 - blocks, D), F32)], 0)
        out[:, :BLK] = rows.T.astype(BF16)
        if extra:
            out[:, BLK : 2 * BLK] = other_vec[...]

    if extra:

        @pl.when(jnp.logical_and(n > 2 * blocks, n < last))
        def _():
            out[...] = other[...]


def ffn_grads(normed, dinner, active, douter, ctx_t, dattend, sums, b1_sum, other=None):
    n = normed.shape[0]
    blocks = FF // D
    extra = 0 if other is None else 3
    width = (2 * blocks + 1 + extra) * D + (2 if extra else 1) * BLK
    part = lambda first, count: (lambda i: (0, jnp.clip(i - first, 0, count - 1)))
    specs = [
        once((n, D)),
        pl.BlockSpec((n, D), part(0, blocks)),
        pl.BlockSpec((n, D), part(blocks, blocks)),
        once((n, D)),
        once((D, n)),
        once((n, D)),
        once((8, D)),
        once((1, FF)),
    ]
    args = [normed, dinner, active, douter, ctx_t, dattend, sums, b1_sum]
    if extra:
        specs += [pl.BlockSpec((D, D), part(2 * blocks + 1, extra)), once((D, BLK), extra * D // BLK)]
        args += [other, other]
    return pl.pallas_call(
        functools.partial(ffn_grads_kernel, extra),
        grid=(2 * blocks + 2 + extra,),
        in_specs=specs,
        out_specs=pl.BlockSpec((D, D), lambda i: (0, i)),
        out_shape=jax.ShapeDtypeStruct((D, width), BF16),
        scratch_shapes=[pltpu.VMEM((D, n), BF16)],
        compiler_params=pltpu.CompilerParams(vmem_limit_bytes=56 * 2**20),
        cost_estimate=cost(1),
        name="ffn_grads",
    )(*args)


def project_kernel(own, low, w, qb, vb, *refs):
    outs = refs if own else refs[4:]
    x = low[...]
    k, k_t, v, v_t = outs[-4:]
    kk = dot(x, w[:, D : 2 * D]).astype(BF16)
    k[...] = kk
    k_t[...] = kk.T
    vv = (dot(x, w[:, 2 * D : 3 * D]) + vb[...]).astype(BF16)
    v[...] = vv
    v_t[...] = vv.T
    if own:
        qq = (dot(x, w[:, :D]) + qb[...]).astype(BF16)
        outs[0][...] = qq
        outs[1][...] = qq.T


def project(rows, w, qb, vb, begun=()):
    own = not begun
    rim = RIM * BLK
    skip = rim // ROWS
    count = rows.shape[0]
    total = count + 2 * rim if own else begun[0].shape[0]
    middle = (total - 2 * rim) // ROWS
    at = (lambda i: i + skip) if own else (lambda i: jnp.where(i < skip, i, i + middle))
    row = pl.BlockSpec((ROWS, D), lambda i: (at(i), 0))
    col = pl.BlockSpec((D, ROWS), lambda i: (0, at(i)))
    plain = pl.BlockSpec((ROWS, D), lambda i: (i, 0))
    turned = pl.BlockSpec((D, ROWS), lambda i: (0, i))
    tall = jax.ShapeDtypeStruct((total, D), BF16)
    wide = jax.ShapeDtypeStruct((D, total), BF16)
    short = [jax.ShapeDtypeStruct((count, D), BF16), jax.ShapeDtypeStruct((D, count), BF16)]
    return pl.pallas_call(
        functools.partial(project_kernel, own),
        grid=(count // ROWS,),
        in_specs=[plain, once((D, 3 * D)), once((1, D)), once((1, D))]
        + [pl.BlockSpec(memory_space=pl.ANY)] * len(begun),
        out_specs=([plain, turned] if own else []) + [row, col, row, col],
        out_shape=(short if own else []) + [tall, wide, tall, wide],
        input_output_aliases={4 + j: j for j in range(len(begun))},
        compiler_params=pltpu.CompilerParams(vmem_limit_bytes=40 * 2**20),
        cost_estimate=cost(8),
        name="project",
    )(rows, w, qb, vb, *begun)


def att_grads_kernel(low, dq_t, dk, dv, dr, rate, out, turned):
    n = pl.program_id(0)
    own = dq_t.shape[1]
    rim = (low.shape[0] - own) // 2

    @pl.when(n == 0)
    def _():
        turned[...] = low[...].T
        out[...] = dot_cols(turned[:, rim : rim + own], dq_t[...]).astype(BF16)

    @pl.when(n == 1)
    def _():
        out[...] = dot(turned[...], dk[...]).astype(BF16)

    @pl.when(n == 2)
    def _():
        out[...] = dot(turned[...], dv[...]).astype(BF16)

    @pl.when(n == 3)
    def _():
        qb = jnp.sum(dq_t[...].astype(F32), 1, keepdims=True)
        vb = jnp.sum(dv[...].astype(F32), 0, keepdims=True)
        left = lax.broadcasted_iota(jnp.int32, (SPAN * SPAN, BLK), 1) < HD
        columns = []
        for hp in range(PAIRS):
            both = dr[:, hp, :]
            columns.append(jnp.sum(jnp.where(left, both, 0.0), 1, keepdims=True))
            columns.append(jnp.sum(jnp.where(left, 0.0, both), 1, keepdims=True))
        logit = jnp.concatenate(columns, 0) * rate[...]
        rows = jnp.concatenate([vb, jnp.zeros((127, D), F32)], 0).T
        lane = lax.broadcasted_iota(jnp.int32, (D, 128), 1)
        out[:, :128] = jnp.where(lane == 2, qb, jnp.where(lane == 1, logit, rows)).astype(BF16)

def att_grads(low_ext, dq_t, dk, dv, dr, rate):
    n = low_ext.shape[0]
    own = dq_t.shape[1]
    return pl.pallas_call(
        att_grads_kernel,
        grid=(4,),
        in_specs=[once((n, D)), once((D, own)), once((n, D)), once((n, D)), once(dr.shape), once((D, 1))],
        out_specs=pl.BlockSpec((D, D), lambda i: (0, i)),
        out_shape=jax.ShapeDtypeStruct((D, 3 * D + 128), BF16),
        scratch_shapes=[pltpu.VMEM((D, n), BF16)],
        compiler_params=pltpu.CompilerParams(vmem_limit_bytes=48 * 2**20),
        cost_estimate=cost(1),
        name="att_grads",
    )(low_ext, dq_t, dk, dv, dr, rate)

def input_back_kernel(dk, dv, dq_t, dfirst, w, own, rims):
    i = pl.program_id(0)
    n = pl.num_programs(0)
    skip = RIM * BLK // ROWS
    total = dot_cols(dk[...], w[:, D : 2 * D]) + dot_cols(dv[...], w[:, 2 * D : 3 * D])
    inside = jnp.logical_and(i >= skip, i < n - skip)

    @pl.when(inside)
    def _():
        own[...] = total + dot_tt(dq_t[...], w[:, :D]) + dfirst[...]

    @pl.when(jnp.logical_not(inside))
    def _():
        rims[...] = total.astype(BF16)

def input_back(dk, dv, dq_t, dfirst, w):
    n = dk.shape[0]
    own = dfirst.shape[0]
    skip = (n - own) // 2 // ROWS
    last = own // ROWS - 1
    row = pl.BlockSpec((ROWS, D), lambda i: (i, 0))
    orow = pl.BlockSpec((ROWS, D), lambda i: (jnp.clip(i - skip, 0, last), 0))
    ocol = pl.BlockSpec((D, ROWS), lambda i: (0, jnp.clip(i - skip, 0, last)))
    rrow = pl.BlockSpec((ROWS, D), lambda i: (jnp.where(i < skip, i, jnp.maximum(i - last - 1, skip)), 0))
    return pl.pallas_call(
        input_back_kernel,
        grid=(n // ROWS,),
        in_specs=[row, row, ocol, orow, once((D, 3 * D))],
        out_specs=[orow, rrow],
        out_shape=[jax.ShapeDtypeStruct((own, D), F32), jax.ShapeDtypeStruct((n - own, D), BF16)],
        compiler_params=pltpu.CompilerParams(vmem_limit_bytes=40 * 2**20),
        cost_estimate=cost(1),
        name="input_back",
    )(dk, dv, dq_t, dfirst, w)


def neighbours(tail, head):
    count = lax.axis_size("dp")
    return (
        lax.ppermute(tail, "dp", [(i, i + 1) for i in range(count - 1)]),
        lax.ppermute(head, "dp", [(i + 1, i) for i in range(count - 1)]),
    )


def gathered(part):
    return lax.all_gather(part, AXES, axis=0, tiled=True)


def place():
    dp = lax.axis_index("dp")
    mp = lax.axis_index("mp")
    return dp // 2, (dp % 2) * (lax.axis_size("mp") // 2) + mp // 2, mp % 2


def sizes():
    return lax.axis_size("dp") // 2, lax.axis_size("mp")


def swap(block, mask):
    count = lax.axis_size("dp") * lax.axis_size("mp")
    return lax.ppermute(block, AXES, [(i, i ^ mask) for i in range(count)])


def put(buffer, piece, index):
    return lax.dynamic_update_slice(buffer, piece[None], (index,) + (0,) * piece.ndim)


class SteppedGather:
    def __init__(self, part):
        self.part = part
        self.block = part
        self.step = 0

    def settle(self, tied):
        if self.step > 0:
            own = place()[self.step - 1]
            out = jnp.zeros((len(self.arriving) + 1,) + self.block.shape, self.block.dtype)
            tied, out = lax.optimization_barrier((tied, out))
            out = put(out, self.block, own)
            for d, piece in self.arriving:
                out = put(out, piece, own ^ d)
            self.block = out
        return tied

    def advance(self, tied):
        far, middle = sizes()
        tied = self.settle(tied)
        tied, self.block = lax.optimization_barrier((tied, self.block))
        self.step += 1
        count, scale = ((far, 2 * middle), (middle, 2), (2, 1))[self.step - 1]
        self.arriving = [(d, swap(self.block, d * scale)) for d in range(1, count)]
        return tied

    def result(self, tied):
        self.settle(tied)
        return self.block.transpose(2, 1, 0, 3, 4).reshape(-1, self.part.shape[1])


def scattered(part):
    return lax.psum_scatter(part, AXES, scatter_dimension=0, tiled=True).astype(F32)


def pick(array, index, axis):
    return lax.dynamic_index_in_dim(array, index, axis, keepdims=False)


class SteppedSum:
    def __init__(self, part):
        far, middle = sizes()
        self.parts = part.reshape(far, middle, 2, -1, part.shape[1])
        self.step = 0

    def anchored(self, tied):
        tied, kept = lax.optimization_barrier((tied, self.halves[0]))
        return tied, (kept, self.halves[1])

    def middle_sum(self, index):
        kept, got = self.halves
        return pick(kept, index, 1).astype(F32) + pick(got, index, 1).astype(F32)

    def far_sum(self, index):
        z, m, c = place()
        total = self.middle_own(index)
        for piece in self.arrived:
            total = total + pick(piece, index, 0).astype(F32)
        return total

    def middle_own(self, index):
        z, m, c = place()
        kept, got = self.halves
        return pick(pick(kept, m, 1), index, 0).astype(F32) + pick(
            pick(got, m, 1), index, 0
        ).astype(F32)

    def advance(self, tied):
        far, middle = sizes()
        z, m, c = place()
        self.step += 1
        if self.step == 1:
            out = pick(self.parts, 1 - c, 2)
            tied, out = lax.optimization_barrier((tied, out))
            self.halves = (pick(self.parts, c, 2), swap(out, 1))
        elif self.step == 2:
            tied, self.halves = self.anchored(tied)
            out = [self.middle_sum(m ^ d).astype(BF16) for d in range(1, middle)]
            tied, out = lax.optimization_barrier((tied, out))
            self.arrived = [swap(item, d * 2) for d, item in zip(range(1, middle), out)]
        else:
            tied, self.halves = self.anchored(tied)
            out = [self.far_sum(z ^ d).astype(BF16) for d in range(1, far)]
            tied, out = lax.optimization_barrier((tied, out))
            self.last = [swap(item, d * 2 * middle) for d, item in zip(range(1, far), out)]
        return tied

    def result(self):
        z, m, c = place()
        total = self.far_sum(z)
        for piece in self.last:
            total = total + piece.astype(F32)
        return total


def table_rows(table):
    rows = table.reshape(PAIRS, 2, SPAN * SPAN).transpose(2, 0, 1)
    return jnp.repeat(rows, BLK, axis=2)


def layer_forward(hidden, low_parts, head, vec, flags, keep, temper, pos, before, between):
    z = (vec["logits"] + vec["jitter"]).reshape(HEADS, SPAN, SPAN) / temper[:, None, None]
    relaxed = jax.nn.sigmoid(z)
    factor = table_rows(relaxed)
    biases = (vec["qb"][None], vec["vb"][None])
    lower, own, upper = low_parts
    low_ext = jnp.concatenate(low_parts, 0)
    q, q_t, *begun = project(own, head, *biases)
    q_t, lower = lax.optimization_barrier((q_t, lower))
    rims = jnp.concatenate([lower, upper], 0)
    k, k_t, v, v_t = project(rims, head, *biases, begun)
    q_t = before(q_t)
    log_factor, inv_factor = jnp.log2(factor), 1.0 / factor
    ctx_t, lse = attend(flags, keep, pos, factor, q_t, k, v_t)
    ctx_t, wo, wo_at, w12 = between(ctx_t)
    names = ("ob", "g1", "s1", "b2", "g2", "s2", "s2", "s2")
    vectors = jnp.stack([vec[name] for name in names])
    first, normed_low, active, slope, second, result, result_low = ffn(
        ctx_t, hidden, wo, wo_at, w12, vectors, vec["b1"][None]
    )
    record = (low_ext, q, q_t, k, k_t, v, ctx_t, lse, first, normed_low, active, slope, second)
    return result, result_low, record + (relaxed, log_factor, inv_factor, vectors, head, wo, wo_at, w12)


def layer_backward(grad, record, flags, keep, temper, pos, before=None, done=None):
    low_ext, q, q_t, k, k_t, v, ctx_t, lse, first, normed_low, active, slope, second = record[:13]
    relaxed, log_factor, inv_factor, vectors, head, wo, wo_at, w12 = record[13:]
    rows = first.shape[0]
    rim = RIM * BLK
    douter, dinner, dfirst, dattend, dc, dc_t, row_sums, b1_sum = ffn_back(
        grad, second, first, slope, w12, wo, wo_at, vectors
    )
    part = ffn_grads(normed_low, dinner, active, douter, ctx_t, dattend, row_sums, b1_sum, before)
    if before is None:
        dc, part = lax.optimization_barrier((dc, part))
        ffn_sum = scattered(part)
    else:
        ffn_sum = SteppedSum(part)
        dc = ffn_sum.advance(dc)
        dc = ffn_sum.advance(dc)
    dq_t, dk, dv, dr = attend_back(
        flags, keep, pos, log_factor, inv_factor, q_t, q, dc_t, dc, ctx_t, lse, k, k_t, v
    )
    rate = ((1.0 - relaxed) / temper[:, None, None]).reshape(-1, 1)
    if before is None:
        own, rims = input_back(dk, dv, dq_t, dfirst, head)
        from_lower, from_upper = neighbours(rims[rim:], rims[:rim])
        dq_t, rims = lax.optimization_barrier((dq_t, rims))
        att_sum = att_grads(low_ext, dq_t, dk, dv, dr, rate)
    else:
        att_sum = SteppedSum(att_grads(low_ext, dq_t, dk, dv, dr, rate))
        dk = att_sum.advance(dk)
        dk, done = lax.optimization_barrier((dk, done))
        dk = ffn_sum.advance(dk)
        own, rims = input_back(dk, dv, dq_t, dfirst, head)
        own = att_sum.advance(own)
        from_lower, from_upper = neighbours(rims[rim:], rims[:rim])
        own = att_sum.advance(own)
    dhidden = own.at[:rim].add(from_lower.astype(F32))
    dhidden = dhidden.at[rows - rim :].add(from_upper.astype(F32))
    return dhidden, ffn_sum, att_sum, done


def per_device(
    embedded,
    opening,
    selector,
    wq,
    wk,
    wv,
    wo,
    qb,
    vb,
    ob,
    g1,
    s1,
    w1,
    b1,
    w2,
    b2,
    g2,
    s2,
    scores,
    jitter,
    warmth,
    upstream,
):
    share = wq.shape[1]
    devices = D // share
    flags = opening[0]
    pos = lax.axis_index("dp").reshape(1).astype(jnp.int32)
    rim = RIM * BLK

    def widened(part):
        lead = part.shape[:-1]
        return jnp.swapaxes(part.reshape(lead + (devices, 4, share)), -3, -2).reshape(lead + (FF,))

    def own_parts(tier):
        narrow = w2[tier].reshape(4, share, D)
        vectors = jnp.stack(
            [item[tier] for item in (qb, vb, ob, g1, s1, b2, g2, s2, scores, jitter)]
            + [b1[tier].reshape(4, share)[j] for j in range(4)],
            1,
        )
        vectors = jnp.pad(vectors, ((0, 0), (0, 128 - vectors.shape[1])))
        first = [wq[tier], wk[tier], wv[tier]]
        wide = [widened(w1[tier])] + [narrow[j] for j in range(4)]
        return first, wide, [wo[tier]], [vectors]

    def unpacked(columns):
        columns = jnp.transpose(columns.astype(F32))
        names = ("qb", "vb", "ob", "g1", "s1", "b2", "g2", "s2", "logits", "jitter")
        vec = {name: columns[n] for n, name in enumerate(names)}
        vec["b1"] = columns[len(names) : len(names) + 4].reshape(FF)
        return vec

    symbols = embedded[0]
    first, wide, out, vectors = own_parts(0)
    gather = SteppedGather(jnp.concatenate(first + vectors, 1))
    symbols = gather.advance(symbols)
    symbols, rest = lax.optimization_barrier((symbols, jnp.concatenate(wide + out, 1)))
    symbols = gather.advance(gather.advance(symbols))
    lower, upper = neighbours(symbols[symbols.shape[0] - rim :], symbols[:rim])
    low_ext = (lower, symbols, upper)
    head_zero = gather.result(symbols)
    head_zero, rest = lax.optimization_barrier((head_zero, rest))
    tail_zero = gathered(rest)
    first, wide, out, vectors = own_parts(1)
    later = SteppedGather(jnp.concatenate(first + out + vectors, 1))
    tails = []

    def between_zero(ctx_t):
        ctx_t = later.advance(ctx_t)
        _, _, *rest = lax.optimization_barrier((ctx_t, tail_zero, *wide))
        tails.append(gathered(jnp.concatenate(rest, 1)))
        return ctx_t, tail_zero, 2 * FF // D, tail_zero

    def between_one(ctx_t):
        return ctx_t, head_one, 3, tails[0]

    hidden, low, record = layer_forward(
        symbols,
        low_ext,
        head_zero,
        unpacked(head_zero[:, 3 * D :]),
        flags,
        selector[0, 0],
        warmth[0],
        pos,
        later.advance,
        between_zero,
    )
    records = [record]
    low = later.advance(low)
    lower, upper = neighbours(low[low.shape[0] - rim :], low[:rim])
    low_ext = (lower, low, upper)
    head_one = later.result(low)
    hidden, _, record = layer_forward(
        hidden,
        low_ext,
        head_one,
        unpacked(head_one[:, 4 * D :]),
        flags,
        selector[1, 0],
        warmth[1],
        pos,
        lambda q_t: q_t,
        between_one,
    )
    records.append(record)
    grad = upstream[0]
    grad, ffn_one, att_one, _ = layer_backward(
        grad, records[1], flags, selector[1, 0], warmth[1], pos
    )
    grad, ffn_zero, att_zero, ffn_one = layer_backward(
        grad, records[0], flags, selector[0, 0], warmth[0], pos, att_one, ffn_one
    )
    both = ffn_zero.result()
    last = att_zero.result()
    ends = [2 * FF + D, 2 * FF + 4 * D]
    fv = jnp.stack([both[:, ends[1] : ends[1] + BLK], ffn_one[:, ends[0] :]])
    av = jnp.stack([last[:, 3 * D :], both[:, ends[1] + BLK :]])
    ffn_sums = jnp.stack([both[:, : ends[0]], ffn_one[:, : ends[0]]])
    att = jnp.stack([last[:, : 3 * D], both[:, ends[0] : ends[1]]])
    w1_grad = unwiden(both, ffn_one)
    w2_grad = jnp.concatenate([ffn_sums[:, :, FF + j * D : FF + (j + 1) * D] for j in range(4)], 1)
    wo_grad = ffn_sums[:, :, 2 * FF :]
    b1_grad = jnp.concatenate([fv[:, :, 8 + j] for j in range(4)], 1)
    new_mask = (scores.astype(F32) + jitter.astype(F32) > 0).astype(jnp.int32)
    return (
        hidden[None],
        grad[None],
        att[:, :, :D],
        att[:, :, D : 2 * D],
        att[:, :, 2 * D : 3 * D],
        wo_grad,
        av[:, :, 2],
        av[:, :, 0],
        fv[:, :, 5],
        fv[:, :, 3],
        fv[:, :, 4],
        w1_grad,
        b1_grad,
        w2_grad,
        fv[:, :, 2],
        fv[:, :, 0],
        fv[:, :, 1],
        av[:, :, 1],
        new_mask,
    )


def solution(mesh):
    rows = P("mp", "dp", None)
    matrix = P(None, AXES, None)
    vector = P(None, AXES)
    return jax.shard_map(
        per_device,
        mesh=mesh,
        in_specs=(rows, P("mp", None), P(None, "mp", "dp", None))
        + (matrix,) * 4
        + (vector,) * 5
        + (matrix, vector, matrix)
        + (vector,) * 5
        + (P(), rows),
        out_specs=(rows, rows)
        + (matrix,) * 4
        + (vector,) * 5
        + (matrix, vector, matrix)
        + (vector,) * 5,
        check_vma=False,
    )
```
